1024 devices in a mesh: pair: 8 (over y), contr: 128 (over x, z, core).
Axes of the slice: x: 4, y: 8, z: 16, core: 2. Of those that a mesh axis runs over, the one named last changes fastest.
Arguments:
- amplitudes: bfloat16 [4096, 131072], P('pair', 'contr'), may hold values from -24 to 24
- integrals: bfloat16 [131072, 1024], P('contr', 'pair'), may hold values from -0.046875 to 0.046875
- occ_irrep: int32 [256], replicated, may hold values from 0 to 7
- virt_irrep: int32 [512], replicated, may hold values from 0 to 7
- occ_energy: float32 [256], replicated, may hold values from -2 to -0.5
- virt_energy: float32 [512], replicated, may hold values from 0.5 to 3
- slab_start: int32 [2], replicated, may hold values from 0 to 496
Outputs:
- update: bfloat16 [4096, 1024], P(('pair', 'contr'))
The draws below stay inside these ranges and needn't reach their ends.
All inputs are finite; a program needn't handle non-finite values.
Results may differ from the reference program's by a relative error of at most 0.003.
Values may be sent and summed in bfloat16 or wider, within the bound.
A program may use at most 64 MiB of HBM per device.

```python
import jax
import jax.numpy as jnp
from jax import lax

VIRT = 512
SLAB = 16
BSLAB = 4
OCC = 256
ROWS = 4096
COLS = 1024
KC = 131072


def plant(result, key, smallest, high):
    longest = result.shape.index(max(result.shape))
    spots = []
    for shift in (0, 1):
        where = [jax.random.randint(jax.random.fold_in(key, axis), (), 0, length) for axis, length in enumerate(result.shape)]
        where[longest] = (where[longest] + shift) % result.shape[longest]
        spots.append(tuple(where))
    return result.at[spots[0]].set(smallest).at[spots[1]].set(high)


def raised(entries, own_key, source, target, parts, factor):
    owner, partner = [(jnp.arange(entries.shape[position]) // (entries.shape[position] // parts)).reshape([-1 if axis == position else 1 for axis in range(entries.ndim)]) for position in (source, target)]
    chosen = jax.random.permutation(own_key, parts)[partner]
    strong = (owner == chosen) | (owner == (partner + parts // 2) % parts)
    return jnp.where(strong, factor * entries, entries)


def block_levels(own_key, shape, cuts, least, high):
    def one(axis_at, blocks):
        steps = jax.random.uniform(jax.random.fold_in(jax.random.fold_in(own_key, 6), axis_at), (blocks,), jnp.float32, least / len(cuts), high / len(cuts))
        return jnp.repeat(jnp.exp(steps), shape[axis_at] // blocks).reshape((-1,) + (1,) * (len(shape) - axis_at - 1))

    loudness = one(*cuts[0])
    for cut in cuts[1:]:
        loudness = loudness * one(*cut)
    return loudness


def bell_draw(rng, dims, width, most, pieces=(), kind=jnp.bfloat16):
    entries = width * jax.random.normal(rng, dims, jnp.float32)
    if pieces:
        entries = entries * block_levels(rng, dims, pieces, -0.22, 0.18)
    return jnp.clip(entries, -most, most).astype(kind)


def bell_draw_with(own_key, dims, scale, reach, pieces, heavy, held_as=jnp.bfloat16):
    result = scale * jax.random.normal(own_key, dims, jnp.float32)
    if pieces:
        result = result * block_levels(own_key, dims, pieces, -0.22, 0.18)
    return jnp.clip(raised(result, jax.random.fold_in(own_key, 3), *heavy), -reach, reach).astype(held_as)


def setup_inputs(seed: int = 0) -> dict:
    streams_of = jax.random.split(jax.random.key(seed), 8)
    amplitudes = bell_draw_with(streams_of[0], (ROWS, KC), 1.0, 24.0, ((0, 8), (1, 128)), (1, 0, 128, 5.5))
    integrals = bell_draw(streams_of[1], (KC, COLS), (KC // 8) ** -0.5, 0.046875, ((0, 128), (1, 8)))
    occ_irrep = plant(jax.random.randint(streams_of[2], (OCC,), 0, 8), jax.random.fold_in(streams_of[2], 1), 0, 7).astype(jnp.int32)
    virt_irrep = plant(jax.random.randint(streams_of[3], (VIRT,), 0, 8), jax.random.fold_in(streams_of[3], 1), 0, 7).astype(jnp.int32)
    occ_energy = jnp.clip(jax.random.uniform(streams_of[4], (OCC,), jnp.float32, -2.0, -0.5), -2.0, -0.5)
    virt_energy = jnp.clip(jax.random.uniform(streams_of[5], (VIRT,), jnp.float32, 0.5, 3.0), 0.5, 3.0)
    slab_start = jax.random.randint(streams_of[6], (2,), 0, VIRT - max(SLAB, BSLAB) + 1).astype(jnp.int32)
    return {"amplitudes": amplitudes, "integrals": integrals, "occ_irrep": occ_irrep, "virt_irrep": virt_irrep, "occ_energy": occ_energy, "virt_energy": virt_energy, "slab_start": slab_start}


def reference(amplitudes, integrals, occ_irrep, virt_irrep, occ_energy, virt_energy, slab_start):
    first_start = slab_start[0].astype(jnp.int32)
    second_start = slab_start[1].astype(jnp.int32)
    a_irrep = lax.dynamic_slice(virt_irrep, (first_start,), (SLAB,))
    b_irrep = lax.dynamic_slice(virt_irrep, (second_start,), (BSLAB,))
    a_energy = lax.dynamic_slice(virt_energy, (first_start,), (SLAB,))
    b_energy = lax.dynamic_slice(virt_energy, (second_start,), (BSLAB,))
    row_irrep = jnp.bitwise_xor(occ_irrep[:, None], a_irrep[None, :]).reshape(-1)
    col_irrep = jnp.bitwise_xor(occ_irrep[:, None], b_irrep[None, :]).reshape(-1)
    row_energy = (occ_energy[:, None] - a_energy[None, :]).reshape(-1)
    col_energy = (occ_energy[:, None] - b_energy[None, :]).reshape(-1)
    zero = jnp.zeros((), jnp.bfloat16)

    def add_block(occupied, total):
        offset = (occupied * VIRT).astype(jnp.int32)
        kc_irrep = jnp.bitwise_xor(occ_irrep[occupied], virt_irrep)
        amp_block = lax.dynamic_slice(amplitudes, (jnp.int32(0), offset), (ROWS, VIRT))
        int_block = lax.dynamic_slice(integrals, (offset, jnp.int32(0)), (VIRT, COLS))
        amp_masked = jnp.where(row_irrep[:, None] == kc_irrep[None, :], amp_block, zero)
        int_masked = jnp.where(kc_irrep[:, None] == col_irrep[None, :], int_block, zero)
        return total + jnp.dot(amp_masked, int_masked, preferred_element_type=jnp.float32)

    cycle = lax.fori_loop(0, OCC, add_block, jnp.zeros((ROWS, COLS), jnp.float32))
    denominator = row_energy[:, None] + col_energy[None, :]
    return (cycle / denominator).astype(jnp.bfloat16)
```

```python
import functools

import jax
import jax.numpy as jnp
from jax import lax
from jax.experimental import pallas as pl
from jax.experimental.pallas import tpu as pltpu
from jax.sharding import PartitionSpec as P

IRREPS = 8
NX = 4
CORES = 2
SLOTS = 32
HIGHEST = lax.Precision.HIGHEST
MESH = pl.DeviceIdType.MESH
NT = (((1,), (1,)), ((), ()))


def iota(shape, axis):
    return lax.broadcasted_iota(jnp.int32, shape, axis)


def ring_order(ny):
    order = [0]
    for step in range(1, ny // 2):
        order += [step, ny - step]
    return order + [ny // 2]


def kernel(
    ny, nx, nz, slots, a_hbm, w_hbm, occ_s, virt_s, occ_en_s, virt_en_s, slab_s, occ_v, virt_v, occ_en_v,
    out_ref, most_ref,
    a_ref, w_ref, gath, part, core_out, core_in, acc, x_in, z_out, z_in, irrep_ref, slot_ref, energy_ref,
    a_sem, w_sem, y_send, y_recv, core_send, core_recv, x_send, x_recv, z_send, z_recv,
):
    me_y = lax.axis_index("pair")
    me_c = lax.axis_index("contr")
    core = me_c % CORES
    me_z = (me_c // CORES) % nz
    me_x = me_c // (CORES * nz)
    rows, depth = a_ref.shape
    cols = w_ref.shape[1]
    half = depth // 2
    occ_count = occ_v.shape[1]
    virt_count = virt_v.shape[1]
    occ_pair = occ_count // ny
    slab_first = rows // occ_pair
    slab_second = cols // occ_pair
    mine = rows // (nx * nz * CORES)
    position = {d: p for p, d in enumerate(ring_order(ny))}
    width = ny // 2 * slots

    copy_w = pltpu.make_async_copy(w_hbm, w_ref, w_sem)
    copy_w.start()
    copy_a = pltpu.make_async_copy(a_hbm, a_ref, a_sem)
    copy_a.start()

    def at(x, z, k):
        return (x * nz + z) * CORES + k

    up = lax.rem(me_y + 1, ny)
    down = lax.rem(me_y + ny - 1, ny)
    other = at(me_x, me_z, 1 - core)

    def x_peer(step):
        return at(lax.rem(me_x + step, nx), me_z, core)

    def z_peer(step):
        return at(me_x, lax.rem(me_z + step, nz), core)

    barrier = pltpu.get_barrier_semaphore()

    def greet(y, c):
        pl.semaphore_signal(barrier, inc=1, device_id=(y, c), device_id_type=MESH)

    greet(up, me_c)
    greet(down, me_c)
    greet(me_y, other)
    for step in range(1, nx):
        greet(me_y, x_peer(step))

    def greet_z(step, carry):
        greet(me_y, z_peer(step))
        return carry

    lax.fori_loop(1, nz, greet_z, 0)

    spread = jnp.where(iota((occ_count, cols), 0) % occ_pair == iota((occ_count, cols), 1) // slab_second, 1.0, 0.0)
    own_row = iota((ny, occ_count), 1) // occ_pair == iota((ny, occ_count), 0)
    b_at = iota((1, cols), 1) % slab_second
    b_irrep = jnp.zeros((1, cols), jnp.int32)
    b_energy = jnp.zeros((1, cols), jnp.float32)
    for b in range(slab_second):
        b_irrep = jnp.where(b_at == b, virt_s[slab_s[1] + b], b_irrep)
        b_energy = jnp.where(b_at == b, virt_en_s[slab_s[1] + b], b_energy)
    occ_row = occ_v[...]
    col_occ = jnp.dot(jnp.where(own_row, occ_row.astype(jnp.float32), 0.0), spread, preferred_element_type=jnp.float32)
    col_irrep = jnp.bitwise_xor(col_occ.astype(jnp.int32), b_irrep)
    col_energy = jnp.dot(
        jnp.where(own_row, occ_en_v[...], 0.0), spread, precision=HIGHEST, preferred_element_type=jnp.float32
    ) - b_energy
    before = jnp.where(iota((cols, cols), 0) < iota((cols, cols), 1), 1.0, 0.0)
    hot = jnp.concatenate([jnp.where(col_irrep == g, 1.0, 0.0) for g in range(IRREPS)], axis=0)
    counted = jnp.dot(hot, before, preferred_element_type=jnp.float32)
    slot = jnp.zeros((ny, cols), jnp.float32)
    for g in range(IRREPS):
        slot = jnp.where(col_irrep == g, counted[g * ny : (g + 1) * ny], slot)
    most_ref[0, 0] = jnp.max(slot)
    slot = slot.astype(jnp.int32)
    irrep_ref[...] = col_irrep
    slot_ref[...] = slot
    energy_ref[...] = col_energy

    local_occ = depth // virt_count
    kc_irrep = jnp.concatenate(
        [jnp.bitwise_xor(virt_v[...], occ_s[me_c * local_occ + k]) for k in range(local_occ)], axis=1
    )

    key = irrep_ref[pl.ds(me_y, 1), :] * slots + slot_ref[pl.ds(me_y, 1), :]
    pick = jnp.where(iota((IRREPS * slots, cols), 0) == key, 1.0, 0.0).astype(jnp.bfloat16)
    copy_w.wait()
    picked = lax.dot_general(pick, w_ref[...], NT, preferred_element_type=jnp.float32)
    kept = picked[:slots]
    for g in range(1, IRREPS):
        kept = jnp.where(kc_irrep == g, picked[g * slots : (g + 1) * slots], kept)
    kept = kept.astype(jnp.bfloat16)
    for h in range(2):
        gath[position[0], h] = kept[:, h * half : (h + 1) * half]

    pl.semaphore_wait(barrier, 3 + (nx - 1) + (nz - 1))

    def y_copy(src, dst, h, to):
        return pltpu.make_async_remote_copy(
            src_ref=gath.at[position[src], h],
            dst_ref=gath.at[position[dst], h],
            send_sem=y_send.at[2 * dst + h],
            recv_sem=y_recv.at[2 * dst + h],
            device_id=(to, me_c),
            device_id_type=MESH,
        )

    y_copies = []

    def forward(dst):
        for turn in range(2):
            for go_down in (True, False):
                d = dst if go_down else ny - dst
                h = turn if go_down else 1 - turn
                src = d - 1 if go_down else (d + 1) % ny
                if dst > 1:
                    y_copy(src, src, h, down).wait_recv()
                if dst == ny // 2 and turn == 1:
                    continue
                copy = y_copy(src, d, h, down if go_down else up)
                copy.start()
                y_copies.append(copy)

    def arrived(dst):
        for h in range(2):
            for d in sorted({dst, ny - dst}):
                y_copy(d, d, h, down).wait_recv()

    def mask_amplitudes():
        a_at = iota((slab_first, 128), 0)
        a_irrep = jnp.zeros((slab_first, 128), jnp.int32)
        for a in range(slab_first):
            a_irrep = jnp.where(a_at == a, virt_s[slab_s[0] + a], a_irrep)
        copy_a.wait()

        def mask(i, carry):
            at_rows = pl.ds(pl.multiple_of(i * slab_first, slab_first), slab_first)
            row_irrep = jnp.bitwise_xor(a_irrep, occ_s[me_y * occ_pair + i])
            row_irrep = jnp.concatenate([row_irrep] * (depth // 128), axis=1)
            block = a_ref[at_rows, :].astype(jnp.float32)
            a_ref[at_rows, :] = jnp.where(row_irrep == kc_irrep, block, 0.0).astype(jnp.bfloat16)
            return carry

        lax.fori_loop(0, occ_pair, mask, 0)

    def multiply(group):
        first = group * ny // 2
        total = None
        for h in range(2):
            block = gath[first : first + ny // 2, h].reshape(width, half)
            product = lax.dot_general(
                a_ref[:, h * half : (h + 1) * half], block, NT, preferred_element_type=jnp.float32
            )
            total = product if total is None else total + product
        part[group] = total
        return send_core(group)

    def strided(group, x, i, k):
        first = (x * nz * CORES + k) * mine + i
        return part[group, pl.ds(first, nz, stride=CORES * mine), :]

    def send_core(group):
        for x in range(nx):
            for i in range(mine):
                core_out[group, x, i * nz : (i + 1) * nz] = strided(group, x, i, 1 - core)
        copy = pltpu.make_async_remote_copy(
            src_ref=core_out.at[group],
            dst_ref=core_in.at[group],
            send_sem=core_send.at[group],
            recv_sem=core_recv.at[group],
            device_id=(me_y, other),
            device_id_type=MESH,
        )
        copy.start()
        for x in range(nx):
            for i in range(mine):
                acc[group, x, i * nz : (i + 1) * nz] = strided(group, x, i, core)
        return copy

    def send_x(group, copy):
        copy.wait_recv()
        acc[group] = acc[group] + core_in[group]
        copies = []
        for step in range(1, nx):
            copies.append(
                pltpu.make_async_remote_copy(
                    src_ref=acc.at[group, lax.rem(me_x + step, nx)],
                    dst_ref=x_in.at[group, step - 1],
                    send_sem=x_send.at[group, step - 1],
                    recv_sem=x_recv.at[group, step - 1],
                    device_id=(me_y, x_peer(step)),
                    device_id_type=MESH,
                )
            )
            copies[-1].start()
        return copies

    def z_copy(group, step):
        return pltpu.make_async_remote_copy(
            src_ref=z_out.at[group, lax.rem(me_z + step, nz)],
            dst_ref=z_in.at[group, step - 1],
            send_sem=z_send.at[group, step - 1],
            recv_sem=z_recv.at[group, step - 1],
            device_id=(me_y, z_peer(step)),
            device_id_type=MESH,
        )

    def send_z(group, copies):
        total = acc[group, me_x]
        for copy in copies:
            copy.wait_recv()
        for step in range(nx - 1):
            total = total + x_in[group, step]
        for i in range(mine):
            z_out[group, :, i, :] = total[i * nz : (i + 1) * nz]

        def go(step, carry):
            z_copy(group, step).start()
            return carry

        lax.fori_loop(1, nz, go, 0)

    def finish(group):
        def ready(step, carry):
            z_copy(group, step).wait_recv()
            return carry

        lax.fori_loop(1, nz, ready, 0)
        total = z_out[group, me_z]
        for step in range(nz - 1):
            total = total + z_in[group, step]
        blocks = [lax.rem(me_y + d, ny) for d in ring_order(ny)[group * ny // 2 : (group + 1) * ny // 2]]
        seat = iota((width, cols), 0)
        place = jnp.concatenate(
            [
                jnp.where(slot_ref[pl.ds(block, 1), :] + p * slots == seat, 1.0, 0.0)
                for p, block in enumerate(blocks)
            ],
            axis=1,
        )
        placed = jnp.dot(total, place, precision=HIGHEST, preferred_element_type=jnp.float32)
        for p, block in enumerate(blocks):
            value = placed[:, p * cols : (p + 1) * cols]
            cycle = jnp.where(row_irrep == irrep_ref[pl.ds(block, 1), :], value, 0.0)
            update = cycle / (row_energy + energy_ref[pl.ds(block, 1), :])
            out_ref[:, pl.ds(pl.multiple_of(block * cols, cols), cols)] = update.astype(out_ref.dtype)

    row_first = me_c * mine
    row_occ = me_y * occ_pair + row_first // slab_first
    row_virt = row_first % slab_first
    row_at = iota((mine, cols), 0)
    row_irrep = jnp.zeros((mine, cols), jnp.int32)
    row_energy = jnp.zeros((mine, cols), jnp.float32)
    for i in range(mine):
        a = slab_s[0] + row_virt + i
        row_irrep = jnp.where(row_at == i, jnp.bitwise_xor(occ_s[row_occ], virt_s[a]), row_irrep)
        row_energy = jnp.where(row_at == i, occ_en_s[row_occ] - virt_en_s[a], row_energy)

    forward(1)
    mask_amplitudes()
    for dst in range(2, ny // 2):
        forward(dst)
    core_first = multiply(0)
    forward(ny // 2)
    x_first = send_x(0, core_first)
    arrived(ny // 2)
    core_second = multiply(1)
    send_z(0, x_first)
    x_second = send_x(1, core_second)
    finish(0)
    send_z(1, x_second)
    finish(1)

    for copy in y_copies + [core_first, core_second] + x_first + x_second:
        copy.wait_send()

    def sent(step, carry):
        for group in range(2):
            z_copy(group, step).wait_send()
        return carry

    lax.fori_loop(1, nz, sent, 0)


def contract(amplitudes, integrals, occ_irrep, virt_irrep, occ_energy, virt_energy, slab_start, slots):
    ny = lax.axis_size("pair")
    nx = NX
    nz = lax.axis_size("contr") // (nx * CORES)
    rows, depth = amplitudes.shape
    cols = integrals.shape[1]
    mine = rows // (nx * nz * CORES)
    width = ny // 2 * slots
    smem = pl.BlockSpec(memory_space=pltpu.SMEM)
    vmem = pl.BlockSpec(memory_space=pltpu.VMEM)
    anywhere = pl.BlockSpec(memory_space=pl.ANY)
    f32 = jnp.float32
    bf16 = jnp.bfloat16
    dma = pltpu.SemaphoreType.DMA
    return pl.pallas_call(
        functools.partial(kernel, ny, nx, nz, slots),
        out_shape=(
            jax.ShapeDtypeStruct((mine, cols * ny), bf16),
            jax.ShapeDtypeStruct((1, 1), f32),
        ),
        in_specs=[anywhere, anywhere] + [smem] * 5 + [vmem] * 3,
        out_specs=(vmem, smem),
        scratch_shapes=[
            pltpu.VMEM((rows, depth), bf16),
            pltpu.VMEM((depth, cols), bf16),
            pltpu.VMEM((ny, 2, slots, depth // 2), bf16),
            pltpu.VMEM((2, rows, width), f32),
            pltpu.VMEM((2, nx, mine * nz, width), f32),
            pltpu.VMEM((2, nx, mine * nz, width), f32),
            pltpu.VMEM((2, nx, mine * nz, width), f32),
            pltpu.VMEM((2, nx - 1, mine * nz, width), f32),
            pltpu.VMEM((2, nz, mine, width), f32),
            pltpu.VMEM((2, nz - 1, mine, width), f32),
            pltpu.VMEM((ny, cols), jnp.int32),
            pltpu.VMEM((ny, cols), jnp.int32),
            pltpu.VMEM((ny, cols), f32),
            dma,
            dma,
            dma((2 * ny,)),
            dma((2 * ny,)),
            dma((2,)),
            dma((2,)),
            dma((2, nx - 1)),
            dma((2, nx - 1)),
            dma((2, nz - 1)),
            dma((2, nz - 1)),
        ],
        compiler_params=pltpu.CompilerParams(
            collective_id=0, has_side_effects=True, vmem_limit_bytes=32 * 1024 * 1024
        ),
        cost_estimate=pl.CostEstimate(
            flops=2 * rows * depth * width * 2, bytes_accessed=2 * depth * (rows + cols), transcendentals=0
        ),
    )(
        amplitudes,
        integrals,
        occ_irrep,
        virt_irrep,
        occ_energy,
        virt_energy,
        slab_start,
        occ_irrep[None, :],
        virt_irrep[None, :],
        occ_energy[None, :],
    )


def dense(amplitudes, integrals, occ_irrep, virt_irrep, occ_energy, virt_energy, slab_start):
    pair_count = lax.axis_size("pair")
    contr_count = lax.axis_size("contr")
    pair_index = lax.axis_index("pair")
    contr_index = lax.axis_index("contr")
    virt_count = virt_irrep.shape[0]
    kc_local = integrals.shape[0]
    occ_local = kc_local // virt_count
    rows_pair = amplitudes.shape[0]
    cols_pair = integrals.shape[1]
    rows_device = rows_pair // contr_count
    slab_first = amplitudes.shape[0] * pair_count // occ_irrep.shape[0]
    slab_second = cols_pair * pair_count // occ_irrep.shape[0]
    a_irrep = lax.dynamic_slice(virt_irrep, (slab_start[0],), (slab_first,))
    b_irrep = lax.dynamic_slice(virt_irrep, (slab_start[1],), (slab_second,))
    a_energy = lax.dynamic_slice(virt_energy, (slab_start[0],), (slab_first,))
    b_energy = lax.dynamic_slice(virt_energy, (slab_start[1],), (slab_second,))
    row_irrep = jnp.bitwise_xor(occ_irrep[:, None], a_irrep[None, :]).reshape(-1)
    col_irrep = jnp.bitwise_xor(occ_irrep[:, None], b_irrep[None, :]).reshape(-1)
    row_energy = (occ_energy[:, None] - a_energy[None, :]).reshape(-1)
    col_energy = (occ_energy[:, None] - b_energy[None, :]).reshape(-1)
    local_occ = lax.dynamic_slice(occ_irrep, (contr_index * occ_local,), (occ_local,))
    kc_irrep = jnp.bitwise_xor(local_occ[:, None], virt_irrep[None, :]).reshape(-1)
    zero = jnp.zeros((), jnp.bfloat16)
    whole_int = lax.all_gather(integrals, "pair", axis=1, tiled=True)
    int_masked = jnp.where(kc_irrep[:, None] == col_irrep[None, :], whole_int, zero)
    row_irrep_pair = lax.dynamic_slice(row_irrep, (pair_index * rows_pair,), (rows_pair,))
    amp_masked = jnp.where(row_irrep_pair[:, None] == kc_irrep[None, :], amplitudes, zero)
    summed = lax.psum_scatter(
        jnp.dot(amp_masked, int_masked, preferred_element_type=jnp.float32),
        "contr",
        scatter_dimension=0,
        tiled=True,
    )
    mine_energy = lax.dynamic_slice(
        row_energy, (pair_index * rows_pair + contr_index * rows_device,), (rows_device,)
    )
    return (summed / (mine_energy[:, None] + col_energy[None, :])).astype(jnp.bfloat16)


def body(*args):
    update, most = contract(*args, slots=SLOTS)
    return lax.cond(most[0, 0] > SLOTS - 1, lambda: dense(*args), lambda: update)


def solution(mesh):
    in_specs = (P("pair", "contr"), P("contr", "pair"), P(), P(), P(), P(), P())
    out_specs = P(("pair", "contr"), None)
    return jax.shard_map(body, mesh=mesh, in_specs=in_specs, out_specs=out_specs, check_vma=False)
```

```python
import functools

import jax
import jax.numpy as jnp
from jax import lax
from jax.experimental import pallas as pl
from jax.experimental.pallas import tpu as pltpu
from jax.sharding import PartitionSpec as P

IRREPS = 8
NX = 4
CORES = 2
SLOTS = 32
HIGHEST = lax.Precision.HIGHEST
MESH = pl.DeviceIdType.MESH
NT = (((1,), (1,)), ((), ()))


def iota(shape, axis):
    return lax.broadcasted_iota(jnp.int32, shape, axis)


def ring_order(ny):
    order = [0]
    for step in range(1, ny // 2):
        order += [step, ny - step]
    return order + [ny // 2]


def kernel(
    ny, nx, nz, slots, a_hbm, w_hbm, occ_hbm, virt_hbm, occ_en_hbm, virt_en_hbm, slab_hbm,
    out_ref, most_ref,
    a_ref, w_ref, occ_s, virt_s, occ_en_s, virt_en_s, slab_s, occ_v, virt_v, occ_en_v,
    gath, part, core_out, core_in, acc, x_in, z_out, z_in, irrep_ref, slot_ref, energy_ref, place_ref,
    in_sem, y_send, y_recv, core_send, core_recv, x_send, x_recv, z_send, z_recv, known_sem,
):
    me_y = lax.axis_index("pair")
    me_c = lax.axis_index("contr")
    core = me_c % CORES
    me_z = (me_c // CORES) % nz
    me_x = me_c // (CORES * nz)
    rows, depth = a_ref.shape
    cols = w_ref.shape[1]
    half = depth // 2
    occ_count = occ_v.shape[1]
    virt_count = virt_v.shape[1]
    occ_pair = occ_count // ny
    slab_first = rows // occ_pair
    slab_second = cols // occ_pair
    mine = rows // (nx * nz * CORES)
    position = {d: p for p, d in enumerate(ring_order(ny))}
    width = ny // 2 * slots

    def at(x, z, k):
        return (x * nz + z) * CORES + k

    other = at(me_x, me_z, 1 - core)

    def x_peer(step):
        return at(lax.rem(me_x + step, nx), me_z, core)

    def z_peer(step):
        return at(me_x, lax.rem(me_z + step, nz), core)

    def near(count, *steps):
        return sorted({step % count for most in steps for step in (most, -most)} - {0})

    barrier = pltpu.get_barrier_semaphore()
    greeted = [(lax.rem(me_y + step, ny), me_c) for step in near(ny, 1, 2)]
    greeted += [(me_y, other)]
    greeted += [(me_y, x_peer(step)) for step in near(nx, 1, 2)]
    greeted += [(me_y, z_peer(step)) for step in near(nz, 1, 2)]
    for device in greeted:
        pl.semaphore_signal(barrier, inc=1, device_id=device, device_id_type=MESH)

    copies_in = [
        pltpu.make_async_copy(src, dst, in_sem.at[i])
        for i, (src, dst) in enumerate(
            [
                (occ_hbm, occ_s),
                (virt_hbm, virt_s),
                (slab_hbm, slab_s),
                (occ_hbm, occ_v),
                (virt_hbm, virt_v),
                (w_hbm, w_ref),
                (a_hbm, a_ref),
                (occ_en_hbm, occ_en_s),
                (virt_en_hbm, virt_en_s),
                (occ_en_hbm, occ_en_v),
            ]
        )
    ]
    for copy in copies_in:
        copy.start()
    copy_w, copy_a = copies_in[5:7]

    relays = []
    reach = 2
    while 2 * reach <= nz // 2:
        relays.append(reach)
        reach *= 2

    def relay(level):
        if level < len(relays):
            for step in near(nz, relays[level]):
                pl.semaphore_signal(
                    known_sem.at[level], inc=1, device_id=(me_y, z_peer(step)), device_id_type=MESH
                )

    def relayed(level):
        if level < len(relays):
            pl.semaphore_wait(known_sem.at[level], len(near(nz, relays[level])))

    spread = jnp.where(iota((occ_count, cols), 0) % occ_pair == iota((occ_count, cols), 1) // slab_second, 1.0, 0.0)
    own_row = iota((ny, occ_count), 1) // occ_pair == iota((ny, occ_count), 0)
    b_at = iota((1, cols), 1) % slab_second
    for copy in copies_in[:5]:
        copy.wait()
    b_irrep = jnp.zeros((1, cols), jnp.int32)
    for b in range(slab_second):
        b_irrep = jnp.where(b_at == b, virt_s[0, slab_s[0, 1] + b], b_irrep)
    occ_row = occ_v[...]
    col_occ = jnp.dot(jnp.where(own_row, occ_row.astype(jnp.float32), 0.0), spread, preferred_element_type=jnp.float32)
    col_irrep = jnp.bitwise_xor(col_occ.astype(jnp.int32), b_irrep)
    before = jnp.where(iota((cols, cols), 0) < iota((cols, cols), 1), 1.0, 0.0)
    hot = jnp.concatenate([jnp.where(col_irrep == g, 1.0, 0.0) for g in range(IRREPS)], axis=0)
    counted = jnp.dot(hot, before, preferred_element_type=jnp.float32)
    slot = jnp.zeros((ny, cols), jnp.float32)
    for g in range(IRREPS):
        slot = jnp.where(col_irrep == g, counted[g * ny : (g + 1) * ny], slot)
    most_ref[0, 0] = jnp.max(slot)
    slot = slot.astype(jnp.int32)
    irrep_ref[...] = col_irrep
    slot_ref[...] = slot

    local_occ = depth // virt_count
    kc_irrep = jnp.concatenate(
        [jnp.bitwise_xor(virt_v[...], occ_s[0, me_c * local_occ + k]) for k in range(local_occ)], axis=1
    )

    key = irrep_ref[pl.ds(me_y, 1), :] * slots + slot_ref[pl.ds(me_y, 1), :]
    pick = jnp.where(iota((IRREPS * slots, cols), 0) == key, 1.0, 0.0).astype(jnp.bfloat16)
    copy_w.wait()
    picked = lax.dot_general(pick, w_ref[...], NT, preferred_element_type=jnp.float32)
    kept = picked[:slots]
    for g in range(1, IRREPS):
        kept = jnp.where(kc_irrep == g, picked[g * slots : (g + 1) * slots], kept)
    kept = kept.astype(jnp.bfloat16)
    for h in range(2):
        gath[position[0], h] = kept[:, h * half : (h + 1) * half]

    pl.semaphore_wait(barrier, len(greeted))

    def y_copy(src, dst, h, step):
        return pltpu.make_async_remote_copy(
            src_ref=gath.at[position[src], h],
            dst_ref=gath.at[position[dst], h],
            send_sem=y_send.at[2 * dst + h],
            recv_sem=y_recv.at[2 * dst + h],
            device_id=(lax.rem(me_y + step % ny, ny), me_c),
            device_id_type=MESH,
        )

    y_copies = []

    def send_y(src, dst, turn):
        for sign in (1, -1):
            h = turn if sign == 1 else 1 - turn
            y_copies.append(y_copy(sign * src % ny, sign * dst % ny, h, sign * (src - dst)))
            y_copies[-1].start()

    def arrived(dst, turns=(0, 1)):
        for turn in turns:
            for sign in (1, -1):
                h = turn if sign == 1 else 1 - turn
                y_copy(sign * dst % ny, sign * dst % ny, h, 1).wait_recv()

    for turn in range(2):
        send_y(0, 2, turn)
        send_y(0, 1, turn)
    relay(0)

    def mask_amplitudes():
        a_at = iota((slab_first, 128), 0)
        a_irrep = jnp.zeros((slab_first, 128), jnp.int32)
        for a in range(slab_first):
            a_irrep = jnp.where(a_at == a, virt_s[0, slab_s[0, 0] + a], a_irrep)
        copy_a.wait()

        def mask(i, carry):
            at_rows = pl.ds(pl.multiple_of(i * slab_first, slab_first), slab_first)
            row_irrep = jnp.bitwise_xor(a_irrep, occ_s[0, me_y * occ_pair + i])
            row_irrep = jnp.concatenate([row_irrep] * (depth // 128), axis=1)
            block = a_ref[at_rows, :].astype(jnp.float32)
            a_ref[at_rows, :] = jnp.where(row_irrep == kc_irrep, block, 0.0).astype(jnp.bfloat16)
            return carry

        lax.fori_loop(0, occ_pair, mask, 0)

    def multiply(group):
        first = group * ny // 2
        total = None
        for h in range(2):
            block = gath[first : first + ny // 2, h].reshape(width, half)
            product = lax.dot_general(
                a_ref[:, h * half : (h + 1) * half], block, NT, preferred_element_type=jnp.float32
            )
            total = product if total is None else total + product
        part[group] = total
        return send_core(group)

    def strided(group, x, i, k):
        first = (x * nz * CORES + k) * mine + i
        return part[group, pl.ds(first, nz, stride=CORES * mine), :]

    def send_core(group):
        for x in range(nx):
            for i in range(mine):
                core_out[group, x, i * nz : (i + 1) * nz] = strided(group, x, i, 1 - core)
        copy = pltpu.make_async_remote_copy(
            src_ref=core_out.at[group],
            dst_ref=core_in.at[group],
            send_sem=core_send.at[group],
            recv_sem=core_recv.at[group],
            device_id=(me_y, other),
            device_id_type=MESH,
        )
        copy.start()
        for x in range(nx):
            for i in range(mine):
                acc[group, x, i * nz : (i + 1) * nz] = strided(group, x, i, core)
        return copy

    def send_x(group, copy):
        copy.wait_recv()
        acc[group] = acc[group] + core_in[group]
        copies = []
        for step in sorted(range(1, nx), key=lambda step: -min(step, nx - step)):
            copies.append(
                pltpu.make_async_remote_copy(
                    src_ref=acc.at[group, lax.rem(me_x + step, nx)],
                    dst_ref=x_in.at[group, step - 1],
                    send_sem=x_send.at[group, step - 1],
                    recv_sem=x_recv.at[group, step - 1],
                    device_id=(me_y, x_peer(step)),
                    device_id_type=MESH,
                )
            )
            copies[-1].start()
        return copies

    def z_copy(group, step):
        return pltpu.make_async_remote_copy(
            src_ref=z_out.at[group, lax.rem(me_z + step, nz)],
            dst_ref=z_in.at[group, step - 1],
            send_sem=z_send.at[group, step - 1],
            recv_sem=z_recv.at[group, step - 1],
            device_id=(me_y, z_peer(step)),
            device_id_type=MESH,
        )

    def send_z(group, copies):
        total = acc[group, me_x]
        for copy in copies:
            copy.wait_recv()
        for step in range(nx - 1):
            total = total + x_in[group, step]
        for i in range(mine):
            z_out[group, :, i, :] = total[i * nz : (i + 1) * nz]

        copies = [z_copy(group, step) for step in sorted(range(1, nz), key=lambda step: -min(step, nz - step))]
        for copy in copies:
            copy.start()
        return copies

    def finish(group, copies):
        for copy in copies:
            copy.wait_recv()
        total = z_out[group, me_z]
        for step in range(nz - 1):
            total = total + z_in[group, step]
        high = total.astype(jnp.bfloat16)
        rest = total - high.astype(jnp.float32)
        middle = rest.astype(jnp.bfloat16)
        low = (rest - middle.astype(jnp.float32)).astype(jnp.bfloat16)
        placed = sum(
            jnp.dot(term, place_ref[group], preferred_element_type=jnp.float32) for term in (low, middle, high)
        )
        blocks = group_blocks(group)
        for p, block in enumerate(blocks):
            value = placed[:, p * cols : (p + 1) * cols]
            cycle = jnp.where(row_irrep == irrep_ref[pl.ds(block, 1), :], value, 0.0)
            update = cycle / (row_energy + energy_ref[pl.ds(block, 1), :])
            out_ref[:, pl.ds(pl.multiple_of(block * cols, cols), cols)] = update.astype(out_ref.dtype)

    def group_blocks(group):
        return [lax.rem(me_y + d, ny) for d in ring_order(ny)[group * ny // 2 : (group + 1) * ny // 2]]

    mask_amplitudes()

    seat = iota((width, cols), 0)
    for group in range(2):
        for p, block in enumerate(group_blocks(group)):
            placing = jnp.where(slot_ref[pl.ds(block, 1), :] + p * slots == seat, 1.0, 0.0)
            place_ref[group, :, p * cols : (p + 1) * cols] = placing.astype(jnp.bfloat16)
    for copy in copies_in[7:]:
        copy.wait()
    b_energy = jnp.zeros((1, cols), jnp.float32)
    for b in range(slab_second):
        b_energy = jnp.where(b_at == b, virt_en_s[0, slab_s[0, 1] + b], b_energy)
    energy_ref[...] = jnp.dot(
        jnp.where(own_row, occ_en_v[...], 0.0), spread, precision=HIGHEST, preferred_element_type=jnp.float32
    ) - b_energy
    row_first = me_c * mine
    row_occ = me_y * occ_pair + row_first // slab_first
    row_virt = row_first % slab_first
    row_at = iota((mine, cols), 0)
    row_irrep = jnp.zeros((mine, cols), jnp.int32)
    row_energy = jnp.zeros((mine, cols), jnp.float32)
    for i in range(mine):
        a = slab_s[0, 0] + row_virt + i
        row_irrep = jnp.where(row_at == i, jnp.bitwise_xor(occ_s[0, row_occ], virt_s[0, a]), row_irrep)
        row_energy = jnp.where(row_at == i, occ_en_s[0, row_occ] - virt_en_s[0, a], row_energy)

    arrived(1, (0,))
    send_y(1, 3, 0)
    arrived(2, (0,))
    send_y(2, 4, 0)
    arrived(1, (1,))
    send_y(1, 3, 1)
    relayed(0)
    relay(1)
    arrived(2, (1,))
    core_first = multiply(0)
    relayed(1)
    x_first = send_x(0, core_first)
    arrived(3)
    arrived(4, (0,))
    core_second = multiply(1)
    z_first = send_z(0, x_first)
    x_second = send_x(1, core_second)
    z_second = send_z(1, x_second)
    finish(0, z_first)
    finish(1, z_second)

    for copy in y_copies + [core_first, core_second] + x_first + x_second + z_first + z_second:
        copy.wait_send()


def contract(amplitudes, integrals, occ_irrep, virt_irrep, occ_energy, virt_energy, slab_start, slots, collective_id=0):
    ny = lax.axis_size("pair")
    nx = NX
    nz = lax.axis_size("contr") // (nx * CORES)
    rows, depth = amplitudes.shape
    cols = integrals.shape[1]
    mine = rows // (nx * nz * CORES)
    width = ny // 2 * slots
    smem = pl.BlockSpec(memory_space=pltpu.SMEM)
    vmem = pl.BlockSpec(memory_space=pltpu.VMEM)
    anywhere = pl.BlockSpec(memory_space=pl.ANY)
    f32 = jnp.float32
    bf16 = jnp.bfloat16
    dma = pltpu.SemaphoreType.DMA
    return pl.pallas_call(
        functools.partial(kernel, ny, nx, nz, slots),
        out_shape=(
            jax.ShapeDtypeStruct((mine, cols * ny), bf16),
            jax.ShapeDtypeStruct((1, 1), f32),
        ),
        in_specs=[anywhere] * 7,
        out_specs=(vmem, smem),
        scratch_shapes=[
            pltpu.VMEM((rows, depth), bf16),
            pltpu.VMEM((depth, cols), bf16),
            pltpu.SMEM((1, occ_irrep.shape[0]), jnp.int32),
            pltpu.SMEM((1, virt_irrep.shape[0]), jnp.int32),
            pltpu.SMEM((1, occ_irrep.shape[0]), f32),
            pltpu.SMEM((1, virt_irrep.shape[0]), f32),
            pltpu.SMEM((1, slab_start.shape[0]), jnp.int32),
            pltpu.VMEM((1, occ_irrep.shape[0]), jnp.int32),
            pltpu.VMEM((1, virt_irrep.shape[0]), jnp.int32),
            pltpu.VMEM((1, occ_irrep.shape[0]), f32),
            pltpu.VMEM((ny, 2, slots, depth // 2), bf16),
            pltpu.VMEM((2, rows, width), f32),
            pltpu.VMEM((2, nx, mine * nz, width), f32),
            pltpu.VMEM((2, nx, mine * nz, width), f32),
            pltpu.VMEM((2, nx, mine * nz, width), f32),
            pltpu.VMEM((2, nx - 1, mine * nz, width), f32),
            pltpu.VMEM((2, nz, mine, width), f32),
            pltpu.VMEM((2, nz - 1, mine, width), f32),
            pltpu.VMEM((ny, cols), jnp.int32),
            pltpu.VMEM((ny, cols), jnp.int32),
            pltpu.VMEM((ny, cols), f32),
            pltpu.VMEM((2, width, ny // 2 * cols), bf16),
            dma((10,)),
            dma((2 * ny,)),
            dma((2 * ny,)),
            dma((2,)),
            dma((2,)),
            dma((2, nx - 1)),
            dma((2, nx - 1)),
            dma((2, nz - 1)),
            dma((2, nz - 1)),
            pltpu.SemaphoreType.REGULAR((2,)),
        ],
        compiler_params=pltpu.CompilerParams(
            collective_id=collective_id, has_side_effects=True, vmem_limit_bytes=32 * 1024 * 1024
        ),
        cost_estimate=pl.CostEstimate(
            flops=2 * rows * depth * width * 2, bytes_accessed=2 * depth * (rows + cols), transcendentals=0
        ),
    )(
        amplitudes,
        integrals,
        occ_irrep[None, :],
        virt_irrep[None, :],
        occ_energy[None, :],
        virt_energy[None, :],
        slab_start[None, :],
    )


def dense(amplitudes, integrals, occ_irrep, virt_irrep, occ_energy, virt_energy, slab_start):
    pair_count = lax.axis_size("pair")
    contr_count = lax.axis_size("contr")
    pair_index = lax.axis_index("pair")
    contr_index = lax.axis_index("contr")
    virt_count = virt_irrep.shape[0]
    kc_local = integrals.shape[0]
    occ_local = kc_local // virt_count
    rows_pair = amplitudes.shape[0]
    cols_pair = integrals.shape[1]
    rows_device = rows_pair // contr_count
    slab_first = amplitudes.shape[0] * pair_count // occ_irrep.shape[0]
    slab_second = cols_pair * pair_count // occ_irrep.shape[0]
    a_irrep = lax.dynamic_slice(virt_irrep, (slab_start[0],), (slab_first,))
    b_irrep = lax.dynamic_slice(virt_irrep, (slab_start[1],), (slab_second,))
    a_energy = lax.dynamic_slice(virt_energy, (slab_start[0],), (slab_first,))
    b_energy = lax.dynamic_slice(virt_energy, (slab_start[1],), (slab_second,))
    row_irrep = jnp.bitwise_xor(occ_irrep[:, None], a_irrep[None, :]).reshape(-1)
    col_irrep = jnp.bitwise_xor(occ_irrep[:, None], b_irrep[None, :]).reshape(-1)
    row_energy = (occ_energy[:, None] - a_energy[None, :]).reshape(-1)
    col_energy = (occ_energy[:, None] - b_energy[None, :]).reshape(-1)
    local_occ = lax.dynamic_slice(occ_irrep, (contr_index * occ_local,), (occ_local,))
    kc_irrep = jnp.bitwise_xor(local_occ[:, None], virt_irrep[None, :]).reshape(-1)
    zero = jnp.zeros((), jnp.bfloat16)
    whole_int = lax.all_gather(integrals, "pair", axis=1, tiled=True)
    int_masked = jnp.where(kc_irrep[:, None] == col_irrep[None, :], whole_int, zero)
    row_irrep_pair = lax.dynamic_slice(row_irrep, (pair_index * rows_pair,), (rows_pair,))
    amp_masked = jnp.where(row_irrep_pair[:, None] == kc_irrep[None, :], amplitudes, zero)
    summed = lax.psum_scatter(
        jnp.dot(amp_masked, int_masked, preferred_element_type=jnp.float32),
        "contr",
        scatter_dimension=0,
        tiled=True,
    )
    mine_energy = lax.dynamic_slice(
        row_energy, (pair_index * rows_pair + contr_index * rows_device,), (rows_device,)
    )
    return (summed / (mine_energy[:, None] + col_energy[None, :])).astype(jnp.bfloat16)


def body(*args):
    update, most = contract(*args, slots=SLOTS)
    return lax.cond(most[0, 0] > SLOTS - 1, lambda: dense(*args), lambda: update)


def solution(mesh):
    in_specs = (P("pair", "contr"), P("contr", "pair"), P(), P(), P(), P(), P())
    out_specs = P(("pair", "contr"), None)
    return jax.shard_map(body, mesh=mesh, in_specs=in_specs, out_specs=out_specs, check_vma=False)
```

```python
import functools

import jax
import jax.numpy as jnp
from jax import lax
from jax.experimental import pallas as pl
from jax.experimental.pallas import tpu as pltpu
from jax.sharding import PartitionSpec as P

IRREPS = 8
NX = 4
CORES = 2
SLOTS = 32
HIGHEST = lax.Precision.HIGHEST
MESH = pl.DeviceIdType.MESH
NT = (((1,), (1,)), ((), ()))


def iota(shape, axis):
    return lax.broadcasted_iota(jnp.int32, shape, axis)


def ring_order(ny):
    order = [0]
    for step in range(1, ny // 2):
        order += [step, ny - step]
    return order + [ny // 2]


def kernel(
    ny, nx, nz, slots, a_hbm, w_hbm, occ_hbm, virt_hbm, occ_en_hbm, virt_en_hbm, slab_hbm,
    out_ref, most_ref,
    a_ref, w_ref, occ_s, virt_s, occ_en_s, virt_en_s, slab_s, occ_v, virt_v, occ_en_v,
    gath, part, core_out, core_in, acc, x_in, z_out, z_in, irrep_ref, slot_ref, energy_ref, place_ref,
    in_sem, y_send, y_recv, core_send, core_recv, x_send, x_recv, z_send, z_recv, known_sem,
):
    me_y = lax.axis_index("pair")
    me_c = lax.axis_index("contr")
    core = me_c % CORES
    me_z = (me_c // CORES) % nz
    me_x = me_c // (CORES * nz)
    rows, depth = a_ref.shape
    cols = w_ref.shape[1]
    half = depth // 2
    occ_count = occ_v.shape[1]
    virt_count = virt_v.shape[1]
    occ_pair = occ_count // ny
    slab_first = rows // occ_pair
    slab_second = cols // occ_pair
    mine = rows // (nx * nz * CORES)
    position = {d: p for p, d in enumerate(ring_order(ny))}
    width = ny // 2 * slots

    def at(x, z, k):
        return (x * nz + z) * CORES + k

    other = at(me_x, me_z, 1 - core)

    def x_peer(step):
        return at(lax.rem(me_x + step, nx), me_z, core)

    def z_peer(step):
        return at(me_x, lax.rem(me_z + step, nz), core)

    def near(count, *steps):
        return sorted({step % count for most in steps for step in (most, -most)} - {0})

    barrier = pltpu.get_barrier_semaphore()
    greeted = [(lax.rem(me_y + step, ny), me_c) for step in near(ny, 1, 2)]
    greeted += [(me_y, other)]
    greeted += [(me_y, x_peer(step)) for step in near(nx, 1, 2)]
    greeted += [(me_y, z_peer(step)) for step in near(nz, 1, 2)]
    for device in greeted:
        pl.semaphore_signal(barrier, inc=1, device_id=device, device_id_type=MESH)

    copies_in = [
        pltpu.make_async_copy(src, dst, in_sem.at[i])
        for i, (src, dst) in enumerate(
            [
                (occ_hbm, occ_s),
                (virt_hbm, virt_s),
                (slab_hbm, slab_s),
                (occ_hbm, occ_v),
                (virt_hbm, virt_v),
                (w_hbm, w_ref),
                (a_hbm, a_ref),
                (occ_en_hbm, occ_en_s),
                (virt_en_hbm, virt_en_s),
                (occ_en_hbm, occ_en_v),
            ]
        )
    ]
    for copy in copies_in:
        copy.start()
    copy_w, copy_a = copies_in[5:7]

    relays = []
    reach = 2
    while 2 * reach <= nz // 2:
        relays.append(reach)
        reach *= 2

    def relay(level):
        if level < len(relays):
            for step in near(nz, relays[level]):
                pl.semaphore_signal(
                    known_sem.at[level], inc=1, device_id=(me_y, z_peer(step)), device_id_type=MESH
                )

    def relayed(level):
        if level < len(relays):
            pl.semaphore_wait(known_sem.at[level], len(near(nz, relays[level])))

    spread = jnp.where(iota((occ_count, cols), 0) % occ_pair == iota((occ_count, cols), 1) // slab_second, 1.0, 0.0)
    own_row = iota((ny, occ_count), 1) // occ_pair == iota((ny, occ_count), 0)
    b_at = iota((1, cols), 1) % slab_second
    for copy in copies_in[:5]:
        copy.wait()
    b_irrep = jnp.zeros((1, cols), jnp.int32)
    for b in range(slab_second):
        b_irrep = jnp.where(b_at == b, virt_s[0, slab_s[0, 1] + b], b_irrep)
    occ_row = occ_v[...]
    col_occ = jnp.dot(jnp.where(own_row, occ_row.astype(jnp.float32), 0.0), spread, preferred_element_type=jnp.float32)
    col_irrep = jnp.bitwise_xor(col_occ.astype(jnp.int32), b_irrep)
    before = jnp.where(iota((cols, cols), 0) < iota((cols, cols), 1), 1.0, 0.0)
    hot = jnp.concatenate([jnp.where(col_irrep == g, 1.0, 0.0) for g in range(IRREPS)], axis=0)
    counted = jnp.dot(hot, before, preferred_element_type=jnp.float32)
    slot = jnp.zeros((ny, cols), jnp.float32)
    for g in range(IRREPS):
        slot = jnp.where(col_irrep == g, counted[g * ny : (g + 1) * ny], slot)
    most_ref[0, 0] = jnp.max(slot)
    slot = slot.astype(jnp.int32)
    irrep_ref[...] = col_irrep
    slot_ref[...] = slot

    local_occ = depth // virt_count
    kc_irrep = jnp.concatenate(
        [jnp.bitwise_xor(virt_v[...], occ_s[0, me_c * local_occ + k]) for k in range(local_occ)], axis=1
    )

    key = irrep_ref[pl.ds(me_y, 1), :] * slots + slot_ref[pl.ds(me_y, 1), :]
    pick = jnp.where(iota((IRREPS * slots, cols), 0) == key, 1.0, 0.0).astype(jnp.bfloat16)
    copy_w.wait()
    picked = lax.dot_general(pick, w_ref[...], NT, preferred_element_type=jnp.float32)
    kept = picked[:slots]
    for g in range(1, IRREPS):
        kept = jnp.where(kc_irrep == g, picked[g * slots : (g + 1) * slots], kept)
    kept = kept.astype(jnp.bfloat16)
    for h in range(2):
        gath[position[0], h] = kept[:, h * half : (h + 1) * half]

    pl.semaphore_wait(barrier, len(greeted))

    def y_copy(src, dst, h, step):
        return pltpu.make_async_remote_copy(
            src_ref=gath.at[position[src], h],
            dst_ref=gath.at[position[dst], h],
            send_sem=y_send.at[2 * dst + h],
            recv_sem=y_recv.at[2 * dst + h],
            device_id=(lax.rem(me_y + step % ny, ny), me_c),
            device_id_type=MESH,
        )

    y_copies = []

    def send_y(src, dst, turn):
        for sign in (1, -1):
            h = turn if sign == 1 else 1 - turn
            y_copies.append(y_copy(sign * src % ny, sign * dst % ny, h, sign * (src - dst)))
            y_copies[-1].start()

    def arrived(dst, turns=(0, 1)):
        for turn in turns:
            for sign in (1, -1):
                h = turn if sign == 1 else 1 - turn
                y_copy(sign * dst % ny, sign * dst % ny, h, 1).wait_recv()

    for turn in range(2):
        send_y(0, 2, turn)
        send_y(0, 1, turn)
    relay(0)

    def mask_amplitudes():
        a_at = iota((slab_first, 128), 0)
        a_irrep = jnp.zeros((slab_first, 128), jnp.int32)
        for a in range(slab_first):
            a_irrep = jnp.where(a_at == a, virt_s[0, slab_s[0, 0] + a], a_irrep)
        copy_a.wait()

        def mask(i, carry):
            at_rows = pl.ds(pl.multiple_of(i * slab_first, slab_first), slab_first)
            row_irrep = jnp.bitwise_xor(a_irrep, occ_s[0, me_y * occ_pair + i])
            row_irrep = jnp.concatenate([row_irrep] * (depth // 128), axis=1)
            block = a_ref[at_rows, :].astype(jnp.float32)
            a_ref[at_rows, :] = jnp.where(row_irrep == kc_irrep, block, 0.0).astype(jnp.bfloat16)
            return carry

        lax.fori_loop(0, occ_pair, mask, 0)

    def multiply(group):
        first = group * ny // 2
        total = None
        for h in range(2):
            block = gath[first : first + ny // 2, h].reshape(width, half)
            product = lax.dot_general(
                a_ref[:, h * half : (h + 1) * half], block, NT, preferred_element_type=jnp.float32
            )
            total = product if total is None else total + product
        for t in range(width // 128):
            part[group, t] = total[:, t * 128 : (t + 1) * 128]
        return send_core(group)

    def strided(group, x, i, k):
        first = (x * nz * CORES + k) * mine + i
        at_rows = pl.ds(first, nz, stride=CORES * mine)
        return jnp.concatenate([part[group, t, at_rows, :] for t in range(width // 128)], axis=1)

    def send_core(group):
        for x in range(nx):
            for i in range(mine):
                core_out[group, x, i * nz : (i + 1) * nz] = strided(group, x, i, 1 - core)
        copy = pltpu.make_async_remote_copy(
            src_ref=core_out.at[group],
            dst_ref=core_in.at[group],
            send_sem=core_send.at[group],
            recv_sem=core_recv.at[group],
            device_id=(me_y, other),
            device_id_type=MESH,
        )
        copy.start()
        for x in range(nx):
            for i in range(mine):
                acc[group, x, i * nz : (i + 1) * nz] = strided(group, x, i, core)
        return copy

    def send_x(group, copy):
        copy.wait_recv()
        acc[group] = acc[group] + core_in[group]
        copies = []
        for step in sorted(range(1, nx), key=lambda step: -min(step, nx - step)):
            copies.append(
                pltpu.make_async_remote_copy(
                    src_ref=acc.at[group, lax.rem(me_x + step, nx)],
                    dst_ref=x_in.at[group, step - 1],
                    send_sem=x_send.at[group, step - 1],
                    recv_sem=x_recv.at[group, step - 1],
                    device_id=(me_y, x_peer(step)),
                    device_id_type=MESH,
                )
            )
            copies[-1].start()
        return copies

    def z_copy(group, step):
        return pltpu.make_async_remote_copy(
            src_ref=z_out.at[group, lax.rem(me_z + step, nz)],
            dst_ref=z_in.at[group, step - 1],
            send_sem=z_send.at[group, step - 1],
            recv_sem=z_recv.at[group, step - 1],
            device_id=(me_y, z_peer(step)),
            device_id_type=MESH,
        )

    def send_z(group, copies):
        total = acc[group, me_x]
        for copy in copies:
            copy.wait_recv()
        for step in range(nx - 1):
            total = total + x_in[group, step]
        for i in range(mine):
            z_out[group, :, i, :] = total[i * nz : (i + 1) * nz]

        copies = [z_copy(group, step) for step in sorted(range(1, nz), key=lambda step: -min(step, nz - step))]
        for copy in copies:
            copy.start()
        return copies

    def finish(group, copies):
        for copy in copies:
            copy.wait_recv()
        total = z_out[group, me_z]
        for step in range(nz - 1):
            total = total + z_in[group, step]
        high = total.astype(jnp.bfloat16)
        rest = total - high.astype(jnp.float32)
        middle = rest.astype(jnp.bfloat16)
        low = (rest - middle.astype(jnp.float32)).astype(jnp.bfloat16)
        placed = sum(
            jnp.dot(term, place_ref[group], preferred_element_type=jnp.float32) for term in (low, middle, high)
        )
        blocks = group_blocks(group)
        for p, block in enumerate(blocks):
            value = placed[:, p * cols : (p + 1) * cols]
            cycle = jnp.where(row_irrep == irrep_ref[pl.ds(block, 1), :], value, 0.0)
            update = cycle / (row_energy + energy_ref[pl.ds(block, 1), :])
            out_ref[:, pl.ds(pl.multiple_of(block * cols, cols), cols)] = update.astype(out_ref.dtype)

    def group_blocks(group):
        return [lax.rem(me_y + d, ny) for d in ring_order(ny)[group * ny // 2 : (group + 1) * ny // 2]]

    mask_amplitudes()

    seat = iota((width, cols), 0)
    for group in range(2):
        for p, block in enumerate(group_blocks(group)):
            placing = jnp.where(slot_ref[pl.ds(block, 1), :] + p * slots == seat, 1.0, 0.0)
            place_ref[group, :, p * cols : (p + 1) * cols] = placing.astype(jnp.bfloat16)
    for copy in copies_in[7:]:
        copy.wait()
    b_energy = jnp.zeros((1, cols), jnp.float32)
    for b in range(slab_second):
        b_energy = jnp.where(b_at == b, virt_en_s[0, slab_s[0, 1] + b], b_energy)
    energy_ref[...] = jnp.dot(
        jnp.where(own_row, occ_en_v[...], 0.0), spread, precision=HIGHEST, preferred_element_type=jnp.float32
    ) - b_energy
    row_first = me_c * mine
    row_occ = me_y * occ_pair + row_first // slab_first
    row_virt = row_first % slab_first
    row_at = iota((mine, cols), 0)
    row_irrep = jnp.zeros((mine, cols), jnp.int32)
    row_energy = jnp.zeros((mine, cols), jnp.float32)
    for i in range(mine):
        a = slab_s[0, 0] + row_virt + i
        row_irrep = jnp.where(row_at == i, jnp.bitwise_xor(occ_s[0, row_occ], virt_s[0, a]), row_irrep)
        row_energy = jnp.where(row_at == i, occ_en_s[0, row_occ] - virt_en_s[0, a], row_energy)

    arrived(1, (0,))
    send_y(1, 3, 0)
    arrived(2, (0,))
    send_y(2, 4, 0)
    arrived(1, (1,))
    send_y(1, 3, 1)
    relayed(0)
    relay(1)
    arrived(2, (1,))
    core_first = multiply(0)
    relayed(1)
    x_first = send_x(0, core_first)
    arrived(3)
    arrived(4, (0,))
    core_second = multiply(1)
    z_first = send_z(0, x_first)
    x_second = send_x(1, core_second)
    z_second = send_z(1, x_second)
    finish(0, z_first)
    finish(1, z_second)

    for copy in y_copies + [core_first, core_second] + x_first + x_second + z_first + z_second:
        copy.wait_send()


def contract(amplitudes, integrals, occ_irrep, virt_irrep, occ_energy, virt_energy, slab_start, slots, collective_id=0):
    ny = lax.axis_size("pair")
    nx = NX
    nz = lax.axis_size("contr") // (nx * CORES)
    rows, depth = amplitudes.shape
    cols = integrals.shape[1]
    mine = rows // (nx * nz * CORES)
    width = ny // 2 * slots
    smem = pl.BlockSpec(memory_space=pltpu.SMEM)
    vmem = pl.BlockSpec(memory_space=pltpu.VMEM)
    hbm = pl.BlockSpec(memory_space=pltpu.HBM)
    f32 = jnp.float32
    bf16 = jnp.bfloat16
    dma = pltpu.SemaphoreType.DMA
    return pl.pallas_call(
        functools.partial(kernel, ny, nx, nz, slots),
        out_shape=(
            jax.ShapeDtypeStruct((mine, cols * ny), bf16),
            jax.ShapeDtypeStruct((1, 1), f32),
        ),
        in_specs=[hbm] * 7,
        out_specs=(vmem, smem),
        scratch_shapes=[
            pltpu.VMEM((rows, depth), bf16),
            pltpu.VMEM((depth, cols), bf16),
            pltpu.SMEM((1, occ_irrep.shape[0]), jnp.int32),
            pltpu.SMEM((1, virt_irrep.shape[0]), jnp.int32),
            pltpu.SMEM((1, occ_irrep.shape[0]), f32),
            pltpu.SMEM((1, virt_irrep.shape[0]), f32),
            pltpu.SMEM((1, slab_start.shape[0]), jnp.int32),
            pltpu.VMEM((1, occ_irrep.shape[0]), jnp.int32),
            pltpu.VMEM((1, virt_irrep.shape[0]), jnp.int32),
            pltpu.VMEM((1, occ_irrep.shape[0]), f32),
            pltpu.VMEM((ny, 2, slots, depth // 2), bf16),
            pltpu.VMEM((2, width // 128, rows, 128), f32),
            pltpu.VMEM((2, nx, mine * nz, width), f32),
            pltpu.VMEM((2, nx, mine * nz, width), f32),
            pltpu.VMEM((2, nx, mine * nz, width), f32),
            pltpu.VMEM((2, nx - 1, mine * nz, width), f32),
            pltpu.VMEM((2, nz, mine, width), f32),
            pltpu.VMEM((2, nz - 1, mine, width), f32),
            pltpu.VMEM((ny, cols), jnp.int32),
            pltpu.VMEM((ny, cols), jnp.int32),
            pltpu.VMEM((ny, cols), f32),
            pltpu.VMEM((2, width, ny // 2 * cols), bf16),
            dma((10,)),
            dma((2 * ny,)),
            dma((2 * ny,)),
            dma((2,)),
            dma((2,)),
            dma((2, nx - 1)),
            dma((2, nx - 1)),
            dma((2, nz - 1)),
            dma((2, nz - 1)),
            pltpu.SemaphoreType.REGULAR((2,)),
        ],
        compiler_params=pltpu.CompilerParams(
            collective_id=collective_id, has_side_effects=True, vmem_limit_bytes=60 * 1024 * 1024
        ),
        cost_estimate=pl.CostEstimate(
            flops=2 * rows * depth * width * 2, bytes_accessed=2 * depth * (rows + cols), transcendentals=0
        ),
    )(
        amplitudes,
        integrals,
        occ_irrep[None, :],
        virt_irrep[None, :],
        occ_energy[None, :],
        virt_energy[None, :],
        slab_start[None, :],
    )


def body(*args):
    update, most = contract(*args, slots=SLOTS, collective_id=0)
    return lax.cond(
        most[0, 0] > SLOTS - 1,
        lambda: contract(*args, slots=args[1].shape[1], collective_id=1)[0],
        lambda: update,
    )


def solution(mesh):
    in_specs = (P("pair", "contr"), P("contr", "pair"), P(), P(), P(), P(), P())
    out_specs = P(("pair", "contr"), None)
    return jax.shard_map(body, mesh=mesh, in_specs=in_specs, out_specs=out_specs, check_vma=False)
```

```python
import functools

import jax
import jax.numpy as jnp
from jax import lax
from jax.experimental import pallas as pl
from jax.experimental.pallas import tpu as pltpu
from jax.sharding import PartitionSpec as P

IRREPS = 8
NX = 4
CORES = 2
SLOTS = 32
HIGHEST = lax.Precision.HIGHEST
MESH = pl.DeviceIdType.MESH
NT = (((1,), (1,)), ((), ()))


def iota(shape, axis):
    return lax.broadcasted_iota(jnp.int32, shape, axis)


def ring_order(ny):
    order = [0]
    for step in range(1, ny // 2):
        order += [step, ny - step]
    return order + [ny // 2]


def kernel(
    ny, nx, nz, slots, a_hbm, w_hbm, occ_hbm, virt_hbm, occ_en_hbm, virt_en_hbm, slab_hbm,
    out_ref, most_ref, occ_v, virt_v, occ_en_v, virt_en_v, slab_v,
    a_ref, w_ref, occ_s, virt_s, occ_en_s, virt_en_s, slab_s,
    gath, part, xc_out, xc_in, z_out, z_in, irrep_ref, slot_ref, energy_ref, place_ref,
    in_sem, y_send, y_recv, xc_send, xc_recv, z_send, z_recv, known_sem,
):
    me_y = lax.axis_index("pair")
    me_c = lax.axis_index("contr")
    core = me_c % CORES
    me_z = (me_c // CORES) % nz
    me_x = me_c // (CORES * nz)
    rows, depth = a_ref.shape
    cols = w_ref.shape[1]
    half = depth // 2
    occ_count = occ_v.shape[1]
    virt_count = virt_v.shape[1]
    occ_pair = occ_count // ny
    slab_first = rows // occ_pair
    slab_second = cols // occ_pair
    mine = rows // (nx * nz * CORES)
    position = {d: p for p, d in enumerate(ring_order(ny))}
    width = ny // 2 * slots

    def at(x, z, k):
        return (x * nz + z) * CORES + k

    other = at(me_x, me_z, 1 - core)

    def x_peer(step):
        return at(lax.rem(me_x + step, nx), me_z, core)

    def z_peer(step):
        return at(me_x, lax.rem(me_z + step, nz), core)

    def near(count, *steps):
        return sorted({step % count for most in steps for step in (most, -most)} - {0}, key=lambda step: -min(step, count - step))

    barrier = pltpu.get_barrier_semaphore()
    greeted = [(lax.rem(me_y + step, ny), me_c) for step in near(ny, 1, 2)]
    greeted += [(me_y, other)]
    greeted += [(me_y, at(lax.rem(me_x + p, nx), me_z, k)) for p in near(nx, 1, 2) for k in (core, 1 - core)]
    greeted += [(me_y, z_peer(step)) for step in near(nz, 1, 2)]
    for device in greeted:
        pl.semaphore_signal(barrier, inc=1, device_id=device, device_id_type=MESH)

    copies_in = [
        pltpu.make_async_copy(src, dst, in_sem.at[i])
        for i, (src, dst) in enumerate(
            [
                (occ_hbm, occ_s),
                (virt_hbm, virt_s),
                (slab_hbm, slab_s),
                (occ_hbm, occ_v),
                (virt_hbm, virt_v),
                (w_hbm, w_ref),
                (a_hbm, a_ref),
                (occ_en_hbm, occ_en_s),
                (virt_en_hbm, virt_en_s),
                (occ_en_hbm, occ_en_v),
                (virt_en_hbm, virt_en_v),
                (slab_hbm, slab_v),
            ]
        )
    ]
    for copy in copies_in:
        copy.start()
    copy_w, copy_a = copies_in[5:7]

    relays = []
    reach = 2
    while 2 * reach <= nz // 2:
        relays.append(reach)
        reach *= 2

    def relay(level):
        if level < len(relays):
            for step in near(nz, relays[level]):
                pl.semaphore_signal(
                    known_sem.at[level], inc=1, device_id=(me_y, z_peer(step)), device_id_type=MESH
                )

    def relayed(level):
        if level < len(relays):
            pl.semaphore_wait(known_sem.at[level], len(near(nz, relays[level])))

    spread = jnp.where(iota((occ_count, cols), 0) % occ_pair == iota((occ_count, cols), 1) // slab_second, 1.0, 0.0)
    own_row = iota((ny, occ_count), 1) // occ_pair == iota((ny, occ_count), 0)
    b_at = iota((1, cols), 1) % slab_second
    for copy in copies_in[:5]:
        copy.wait()
    b_irrep = jnp.zeros((1, cols), jnp.int32)
    for b in range(slab_second):
        b_irrep = jnp.where(b_at == b, virt_s[0, slab_s[0, 1] + b], b_irrep)
    occ_row = occ_v[...]
    col_occ = jnp.dot(jnp.where(own_row, occ_row.astype(jnp.float32), 0.0), spread, preferred_element_type=jnp.float32)
    col_irrep = jnp.bitwise_xor(col_occ.astype(jnp.int32), b_irrep)
    before = jnp.where(iota((cols, cols), 0) < iota((cols, cols), 1), 1.0, 0.0)
    hot = jnp.concatenate([jnp.where(col_irrep == g, 1.0, 0.0) for g in range(IRREPS)], axis=0)
    counted = jnp.dot(hot, before, preferred_element_type=jnp.float32)
    slot = jnp.zeros((ny, cols), jnp.float32)
    for g in range(IRREPS):
        slot = jnp.where(col_irrep == g, counted[g * ny : (g + 1) * ny], slot)
    most_ref[0, 0] = jnp.max(slot)
    slot = slot.astype(jnp.int32)
    irrep_ref[...] = col_irrep
    slot_ref[...] = slot

    local_occ = depth // virt_count
    kc_irrep = jnp.concatenate(
        [jnp.bitwise_xor(virt_v[...], occ_s[0, me_c * local_occ + k]) for k in range(local_occ)], axis=1
    )

    key = irrep_ref[pl.ds(me_y, 1), :] * slots + slot_ref[pl.ds(me_y, 1), :]
    pick = jnp.where(iota((IRREPS * slots, cols), 0) == key, 1.0, 0.0).astype(jnp.bfloat16)
    copy_w.wait()
    picked = lax.dot_general(pick, w_ref[...], NT, preferred_element_type=jnp.float32)
    kept = picked[:slots]
    for g in range(1, IRREPS):
        kept = jnp.where(kc_irrep == g, picked[g * slots : (g + 1) * slots], kept)
    kept = kept.astype(jnp.bfloat16)
    for h in range(2):
        gath[position[0], h] = kept[:, h * half : (h + 1) * half]

    pl.semaphore_wait(barrier, len(greeted))

    def y_copy(src, dst, h, step):
        return pltpu.make_async_remote_copy(
            src_ref=gath.at[position[src], h],
            dst_ref=gath.at[position[dst], h],
            send_sem=y_send.at[2 * dst + h],
            recv_sem=y_recv.at[2 * dst + h],
            device_id=(lax.rem(me_y + step % ny, ny), me_c),
            device_id_type=MESH,
        )

    y_copies = []

    def send_y(src, dst, turn):
        for sign in (1, -1):
            h = turn if sign == 1 else 1 - turn
            y_copies.append(y_copy(sign * src % ny, sign * dst % ny, h, sign * (src - dst)))
            y_copies[-1].start()

    def arrived(dst, turns=(0, 1)):
        for turn in turns:
            for sign in (1, -1):
                h = turn if sign == 1 else 1 - turn
                y_copy(sign * dst % ny, sign * dst % ny, h, 1).wait_recv()

    send_y(0, 2, 0)
    send_y(0, 2, 1)
    send_y(0, 1, 0)
    send_y(0, 1, 1)
    relay(0)

    def mask_amplitudes():
        a_at = iota((slab_first, 128), 0)
        a_irrep = jnp.zeros((slab_first, 128), jnp.int32)
        for a in range(slab_first):
            a_irrep = jnp.where(a_at == a, virt_s[0, slab_s[0, 0] + a], a_irrep)
        copy_a.wait()

        def mask(i, carry):
            at_rows = pl.ds(pl.multiple_of(i * slab_first, slab_first), slab_first)
            row_irrep = jnp.bitwise_xor(a_irrep, occ_s[0, me_y * occ_pair + i])
            row_irrep = jnp.concatenate([row_irrep] * (depth // 128), axis=1)
            block = a_ref[at_rows, :].astype(jnp.float32)
            a_ref[at_rows, :] = jnp.where(row_irrep == kc_irrep, block, 0.0).astype(jnp.bfloat16)
            return carry

        lax.fori_loop(0, occ_pair, mask, 0)

    def multiply(group):
        first = group * ny // 2
        total = None
        for h in range(2):
            block = gath[first : first + ny // 2, h].reshape(width, half)
            product = lax.dot_general(
                a_ref[:, h * half : (h + 1) * half], block, NT, preferred_element_type=jnp.float32
            )
            total = product if total is None else total + product
        for t in range(width // 128):
            part[group, t] = total[:, t * 128 : (t + 1) * 128]
        return send_xc(group)

    def strided(group, x, i, k):
        first = (x * nz * CORES + k) * mine + i
        at_rows = pl.ds(first, nz, stride=CORES * mine)
        return jnp.concatenate([part[group, t, at_rows, :] for t in range(width // 128)], axis=1)

    def send_xc(group):
        for x in range(nx):
            for k in range(CORES):
                for i in range(mine):
                    rows_i = strided(group, x, i, k).astype(xc_out.dtype)
                    xc_out[group, x * CORES + k, i * nz : (i + 1) * nz] = rows_i
        copies = []
        for p in sorted(range(nx), key=lambda step: -min(step, nx - step)):
            for q in range(CORES):
                if p or q:
                    x, k = lax.rem(me_x + p, nx), lax.rem(core + q, CORES)
                    copies.append(
                        pltpu.make_async_remote_copy(
                            src_ref=xc_out.at[group, x * CORES + k],
                            dst_ref=xc_in.at[group, p * CORES + q - 1],
                            send_sem=xc_send.at[group, p * CORES + q - 1],
                            recv_sem=xc_recv.at[group, p * CORES + q - 1],
                            device_id=(me_y, at(x, me_z, k)),
                            device_id_type=MESH,
                        )
                    )
                    copies[-1].start()
        return copies

    def z_copy(group, step):
        return pltpu.make_async_remote_copy(
            src_ref=z_out.at[group, lax.rem(me_z + step, nz)],
            dst_ref=z_in.at[group, step - 1],
            send_sem=z_send.at[group, step - 1],
            recv_sem=z_recv.at[group, step - 1],
            device_id=(me_y, z_peer(step)),
            device_id_type=MESH,
        )

    def send_z(group, copies):
        total = jnp.concatenate([strided(group, me_x, i, core) for i in range(mine)], axis=0)
        for copy in copies:
            copy.wait_recv()
        for step in range(nx * CORES - 1):
            total = total + xc_in[group, step].astype(jnp.float32)
        for i in range(mine):
            z_out[group, :, i, :] = total[i * nz : (i + 1) * nz]

        copies = [z_copy(group, step) for step in sorted(range(1, nz), key=lambda step: -min(step, nz - step))]
        for copy in copies:
            copy.start()
        return copies

    def finish(group, copies):
        for copy in copies:
            copy.wait_recv()
        total = z_out[group, me_z]
        for step in range(nz - 1):
            total = total + z_in[group, step]
        high = total.astype(jnp.bfloat16)
        rest = total - high.astype(jnp.float32)
        middle = rest.astype(jnp.bfloat16)
        low = (rest - middle.astype(jnp.float32)).astype(jnp.bfloat16)
        placed = sum(
            jnp.dot(term, place_ref[group], preferred_element_type=jnp.float32) for term in (low, middle, high)
        )
        blocks = group_blocks(group)
        for p, block in enumerate(blocks):
            value = placed[:, p * cols : (p + 1) * cols]
            cycle = jnp.where(row_irrep == irrep_ref[pl.ds(block, 1), :], value, 0.0)
            update = cycle / (row_energy + energy_ref[pl.ds(block, 1), :])
            out_ref[:, pl.ds(pl.multiple_of(block * cols, cols), cols)] = update.astype(out_ref.dtype)

    def group_blocks(group):
        return [lax.rem(me_y + d, ny) for d in ring_order(ny)[group * ny // 2 : (group + 1) * ny // 2]]

    mask_amplitudes()

    seat = iota((width, cols), 0)
    for group in range(2):
        for p, block in enumerate(group_blocks(group)):
            placing = jnp.where(slot_ref[pl.ds(block, 1), :] + p * slots == seat, 1.0, 0.0)
            place_ref[group, :, p * cols : (p + 1) * cols] = placing.astype(jnp.bfloat16)
    for copy in copies_in[7:]:
        copy.wait()
    b_energy = jnp.zeros((1, cols), jnp.float32)
    for b in range(slab_second):
        b_energy = jnp.where(b_at == b, virt_en_s[0, slab_s[0, 1] + b], b_energy)
    energy_ref[...] = jnp.dot(
        jnp.where(own_row, occ_en_v[...], 0.0), spread, precision=HIGHEST, preferred_element_type=jnp.float32
    ) - b_energy
    row_first = me_c * mine
    row_occ = me_y * occ_pair + row_first // slab_first
    row_virt = row_first % slab_first
    row_at = iota((mine, cols), 0)
    row_irrep = jnp.zeros((mine, cols), jnp.int32)
    row_energy = jnp.zeros((mine, cols), jnp.float32)
    for i in range(mine):
        a = slab_s[0, 0] + row_virt + i
        row_irrep = jnp.where(row_at == i, jnp.bitwise_xor(occ_s[0, row_occ], virt_s[0, a]), row_irrep)
        row_energy = jnp.where(row_at == i, occ_en_s[0, row_occ] - virt_en_s[0, a], row_energy)

    arrived(2, (0,))
    send_y(2, 4, 0)
    send_y(2, 3, 0)
    arrived(2, (1,))
    send_y(2, 3, 1)
    relayed(0)
    relay(1)
    arrived(1)
    x_first = multiply(0)
    relayed(1)
    arrived(3)
    arrived(4, (0,))
    x_second = multiply(1)
    z_first = send_z(0, x_first)
    z_second = send_z(1, x_second)
    finish(0, z_first)
    finish(1, z_second)

    for copy in y_copies + x_first + x_second + z_first + z_second:
        copy.wait_send()


def contract(amplitudes, integrals, *small, slots, collective_id=0):
    ny = lax.axis_size("pair")
    nx = NX
    nz = lax.axis_size("contr") // (nx * CORES)
    rows, depth = amplitudes.shape
    cols = integrals.shape[1]
    mine = rows // (nx * nz * CORES)
    width = ny // 2 * slots
    vmem = pl.BlockSpec(memory_space=pltpu.VMEM)
    hbm = pl.BlockSpec(memory_space=pltpu.HBM)
    f32 = jnp.float32
    bf16 = jnp.bfloat16
    dma = pltpu.SemaphoreType.DMA
    return pl.pallas_call(
        functools.partial(kernel, ny, nx, nz, slots),
        out_shape=(
            jax.ShapeDtypeStruct((mine, cols * ny), bf16),
            jax.ShapeDtypeStruct((1, 1), f32),
            *(jax.ShapeDtypeStruct(array.shape, array.dtype) for array in small),
        ),
        in_specs=[hbm] * 7,
        out_specs=(vmem, pl.BlockSpec(memory_space=pltpu.SMEM)) + (vmem,) * 5,
        scratch_shapes=[
            pltpu.VMEM((rows, depth), bf16),
            pltpu.VMEM((depth, cols), bf16),
            *(pltpu.SMEM(array.shape, array.dtype) for array in small),
            pltpu.VMEM((ny, 2, slots, depth // 2), bf16),
            pltpu.VMEM((2, width // 128, rows, 128), f32),
            pltpu.VMEM((2, nx * CORES, mine * nz, width), f32),
            pltpu.VMEM((2, nx * CORES - 1, mine * nz, width), f32),
            pltpu.VMEM((2, nz, mine, width), f32),
            pltpu.VMEM((2, nz - 1, mine, width), f32),
            pltpu.VMEM((ny, cols), jnp.int32),
            pltpu.VMEM((ny, cols), jnp.int32),
            pltpu.VMEM((ny, cols), f32),
            pltpu.VMEM((2, width, ny // 2 * cols), bf16),
            dma((12,)),
            dma((2 * ny,)),
            dma((2 * ny,)),
            dma((2, nx * CORES - 1)),
            dma((2, nx * CORES - 1)),
            dma((2, nz - 1)),
            dma((2, nz - 1)),
            pltpu.SemaphoreType.REGULAR((2,)),
        ],
        compiler_params=pltpu.CompilerParams(
            collective_id=collective_id, has_side_effects=True, vmem_limit_bytes=60 * 1024 * 1024
        ),
        cost_estimate=pl.CostEstimate(
            flops=2 * rows * depth * width * 2, bytes_accessed=2 * depth * (rows + cols), transcendentals=0
        ),
    )(amplitudes, integrals, *small)


def body(amplitudes, integrals, *small):
    small = [array[None, :] for array in small]
    update, most, *small = contract(amplitudes, integrals, *small, slots=SLOTS, collective_id=0)
    return lax.cond(
        most[0, 0] > SLOTS - 1,
        lambda: contract(amplitudes, integrals, *small, slots=integrals.shape[1], collective_id=1)[0],
        lambda: update,
    )


def solution(mesh):
    in_specs = (P("pair", "contr"), P("contr", "pair"), P(), P(), P(), P(), P())
    out_specs = P(("pair", "contr"), None)
    return jax.shard_map(body, mesh=mesh, in_specs=in_specs, out_specs=out_specs, check_vma=False)
```

```python
import functools

import jax
import jax.numpy as jnp
from jax import lax
from jax.experimental import pallas as pl
from jax.experimental.pallas import tpu as pltpu
from jax.sharding import PartitionSpec as P

IRREPS = 8
NX = 4
CORES = 2
SLOTS = 32
HIGHEST = lax.Precision.HIGHEST
MESH = pl.DeviceIdType.MESH
NT = (((1,), (1,)), ((), ()))


def iota(shape, axis):
    return lax.broadcasted_iota(jnp.int32, shape, axis)


def ring_order(ny):
    order = [0]
    for step in range(1, ny // 2):
        order += [step, ny - step]
    return order + [ny // 2]


def kernel(
    ny, nx, nz, slots, a_hbm, w_hbm, occ_hbm, virt_hbm, occ_en_hbm, virt_en_hbm, slab_hbm,
    out_ref, most_hbm, occ_v, virt_v, occ_en_v, virt_en_v, slab_v,
    most_ref, a_ref, w_ref, occ_s, virt_s, occ_en_s, virt_en_s, slab_s,
    gath, part, xc_out, xc_in, z_out, z_in, irrep_ref, slot_ref, energy_ref, place_ref,
    in_sem, y_send, y_recv, xc_send, xc_recv, z_send, z_recv, known_sem,
):
    me_y = lax.axis_index("pair")
    me_c = lax.axis_index("contr")
    core = me_c % CORES
    me_z = (me_c // CORES) % nz
    me_x = me_c // (CORES * nz)
    rows, depth = a_ref.shape
    cols = w_ref.shape[1]
    half = depth // 2
    occ_count = occ_v.shape[1]
    virt_count = virt_v.shape[1]
    occ_pair = occ_count // ny
    slab_first = rows // occ_pair
    slab_second = cols // occ_pair
    mine = rows // (nx * nz * CORES)
    position = {d: p for p, d in enumerate(ring_order(ny))}
    width = ny // 2 * slots
    rows_x = rows // nx

    def at(x, z, k):
        return (x * nz + z) * CORES + k

    other = at(me_x, me_z, 1 - core)

    def x_peer(step):
        return at(lax.rem(me_x + step, nx), me_z, core)

    def z_peer(step):
        return at(me_x, lax.rem(me_z + step, nz), core)

    def near(count, *steps):
        return sorted({step % count for most in steps for step in (most, -most)} - {0}, key=lambda step: -min(step, count - step))

    barrier = pltpu.get_barrier_semaphore()
    greeted = [(lax.rem(me_y + step, ny), me_c) for step in near(ny, 1, 2)]
    greeted += [(me_y, other)]
    greeted += [(me_y, x_peer(step)) for step in near(nx, 1)]
    greeted += [(me_y, z_peer(step)) for step in near(nz, 1)]

    copies_in = [
        pltpu.make_async_copy(src, dst, in_sem.at[i])
        for i, (src, dst) in enumerate(
            [
                (occ_hbm, occ_v),
                (virt_hbm, virt_v),
                (slab_hbm, slab_s),
                (virt_hbm, virt_s),
                (occ_hbm, occ_s),
                (w_hbm, w_ref),
                (a_hbm, a_ref),
                (occ_en_hbm, occ_en_s),
                (virt_en_hbm, virt_en_s),
                (occ_en_hbm, occ_en_v),
                (virt_en_hbm, virt_en_v),
                (slab_hbm, slab_v),
            ]
        )
    ]
    for copy in copies_in:
        copy.start()
    copy_a = copies_in[6]

    for device in greeted:
        pl.semaphore_signal(barrier, inc=1, device_id=device, device_id_type=MESH)

    relays = [[x_peer(step) for step in near(nx, 1)], [other]]
    reach, level = 1, 0
    while 2 * reach <= nz // 2:
        relays += [[]] * (level == len(relays))
        relays[level] = relays[level] + [z_peer(step) for step in near(nz, reach)]
        reach, level = 2 * reach, level + 1
    last = len(relays) - 1

    def relay(level):
        for peer in relays[level]:
            pl.semaphore_signal(known_sem.at[level], inc=1, device_id=(me_y, peer), device_id_type=MESH)

    def relayed(level):
        pl.semaphore_wait(known_sem.at[level], len(relays[level]))

    own_spread = jnp.where(
        iota((occ_count, cols), 0) == me_y * occ_pair + iota((occ_count, cols), 1) // slab_second, 1.0, 0.0
    )
    before = jnp.where(iota((cols, cols), 0) < iota((cols, cols), 1), 1.0, 0.0)
    b_at = iota((1, cols), 1) % slab_second
    for copy in copies_in[:6]:
        copy.wait()
    b_irrep = jnp.zeros((1, cols), jnp.int32)
    for b in range(slab_second):
        b_irrep = jnp.where(b_at == b, virt_s[0, slab_s[0, 1] + b], b_irrep)
    occ_row = occ_v[...].astype(jnp.float32)
    own_occ = jnp.dot(occ_row, own_spread, preferred_element_type=jnp.float32)
    own_irrep = jnp.bitwise_xor(own_occ.astype(jnp.int32), b_irrep)
    own_hot = jnp.where(own_irrep == iota((IRREPS, cols), 0), 1.0, 0.0)
    own_counted = jnp.dot(own_hot, before, preferred_element_type=jnp.float32)
    own_slot = jnp.sum(own_hot * own_counted, axis=0, keepdims=True).astype(jnp.int32)
    local_occ = depth // virt_count
    kc_irrep = jnp.concatenate(
        [jnp.bitwise_xor(virt_v[...], occ_s[0, me_c * local_occ + k]) for k in range(local_occ)], axis=1
    )
    key = own_irrep * slots + own_slot
    pick = jnp.where(iota((IRREPS * slots, cols), 0) == key, 1.0, 0.0).astype(jnp.bfloat16)
    picked = lax.dot_general(pick, w_ref[...], NT, preferred_element_type=jnp.float32)
    kept = picked[:slots]
    for g in range(1, IRREPS):
        kept = jnp.where(kc_irrep == g, picked[g * slots : (g + 1) * slots], kept)
    kept = kept.astype(jnp.bfloat16)
    for h in range(2):
        gath[position[0], h] = kept[:, h * half : (h + 1) * half]

    pl.semaphore_wait(barrier, len(greeted))

    def y_copy(src, dst, h, step):
        return pltpu.make_async_remote_copy(
            src_ref=gath.at[position[src], h],
            dst_ref=gath.at[position[dst], h],
            send_sem=y_send.at[2 * dst + h],
            recv_sem=y_recv.at[2 * dst + h],
            device_id=(lax.rem(me_y + step % ny, ny), me_c),
            device_id_type=MESH,
        )

    y_copies = []

    def send_y(src, dst, turn):
        for sign in (1, -1):
            h = turn if sign == 1 else 1 - turn
            y_copies.append(y_copy(sign * src % ny, sign * dst % ny, h, sign * (src - dst)))
            y_copies[-1].start()

    def arrived(dst, turns=(0, 1)):
        for turn in turns:
            for sign in (1, -1):
                h = turn if sign == 1 else 1 - turn
                y_copy(sign * dst % ny, sign * dst % ny, h, 1).wait_recv()

    send_y(0, 2, 0)
    send_y(0, 2, 1)
    send_y(0, 1, 0)
    send_y(0, 1, 1)
    relay(0)

    def mask_amplitudes():
        a_at = iota((slab_first, 128), 0)
        a_irrep = jnp.zeros((slab_first, 128), jnp.int32)
        for a in range(slab_first):
            a_irrep = jnp.where(a_at == a, virt_s[0, slab_s[0, 0] + a], a_irrep)
        copy_a.wait()

        def mask(i, carry):
            at_rows = pl.ds(pl.multiple_of(i * slab_first, slab_first), slab_first)
            row_irrep = jnp.bitwise_xor(a_irrep, occ_s[0, me_y * occ_pair + i])
            row_irrep = jnp.concatenate([row_irrep] * (depth // 128), axis=1)
            block = a_ref[at_rows, :].astype(jnp.float32)
            a_ref[at_rows, :] = jnp.where(row_irrep == kc_irrep, block, 0.0).astype(jnp.bfloat16)
            return carry

        lax.fori_loop(0, occ_pair, mask, 0)

    def far_first(count):
        return sorted(range(count), key=lambda step: -min(step, count - step))

    def multiply(group):
        first = group * ny // 2
        blocks = [gath[first : first + ny // 2, h].reshape(width, half) for h in range(2)]
        copies = []
        for p in far_first(nx):
            x = lax.rem(me_x + p, nx)
            at_rows = pl.ds(pl.multiple_of(x * rows_x, rows_x), rows_x)
            total = sum(
                lax.dot_general(
                    a_ref[at_rows, h * half : (h + 1) * half], blocks[h], NT, preferred_element_type=jnp.float32
                )
                for h in range(2)
            )
            for t in range(width // 128):
                part[group, p, t] = total[:, t * 128 : (t + 1) * 128]
            for k in range(CORES):
                for i in range(mine):
                    xc_out[group, p * CORES + k, i * nz : (i + 1) * nz] = strided(group, p, i, k)
            for q in range(CORES):
                if p or q:
                    k = lax.rem(core + q, CORES)
                    copies.append(
                        pltpu.make_async_remote_copy(
                            src_ref=xc_out.at[group, p * CORES + k],
                            dst_ref=xc_in.at[group, p * CORES + q - 1],
                            send_sem=xc_send.at[group, p * CORES + q - 1],
                            recv_sem=xc_recv.at[group, p * CORES + q - 1],
                            device_id=(me_y, at(x, me_z, k)),
                            device_id_type=MESH,
                        )
                    )
                    copies[-1].start()
        return copies

    def strided(group, p, i, k):
        at_rows = pl.ds(k * mine + i, nz, stride=CORES * mine)
        return jnp.concatenate([part[group, p, t, at_rows, :] for t in range(width // 128)], axis=1)

    def z_copy(group, step):
        return pltpu.make_async_remote_copy(
            src_ref=z_out.at[group, lax.rem(me_z + step, nz)],
            dst_ref=z_in.at[group, step - 1],
            send_sem=z_send.at[group, step - 1],
            recv_sem=z_recv.at[group, step - 1],
            device_id=(me_y, z_peer(step)),
            device_id_type=MESH,
        )

    def send_z(group, copies):
        total = xc_out[group, core]
        for copy in copies:
            copy.wait_recv()
        for step in range(nx * CORES - 1):
            total = total + xc_in[group, step].astype(jnp.float32)
        for i in range(mine):
            z_out[group, :, i, :] = total[i * nz : (i + 1) * nz]

        copies = [z_copy(group, step) for step in sorted(range(1, nz), key=lambda step: -min(step, nz - step))]
        for copy in copies:
            copy.start()
        return copies

    def finish(group, copies):
        for copy in copies:
            copy.wait_recv()
        total = z_out[group, me_z]
        for step in range(nz - 1):
            total = total + z_in[group, step]
        high = total.astype(jnp.bfloat16)
        rest = total - high.astype(jnp.float32)
        middle = rest.astype(jnp.bfloat16)
        low = (rest - middle.astype(jnp.float32)).astype(jnp.bfloat16)
        terms = jnp.concatenate([term.astype(jnp.float32) for term in (low, middle, high)], axis=0).astype(jnp.bfloat16)
        placed = jnp.dot(terms, place_ref[group], preferred_element_type=jnp.float32)
        placed = placed[:mine] + placed[mine : 2 * mine] + placed[2 * mine :]
        blocks = group_blocks(group)
        for p, block in enumerate(blocks):
            value = placed[:, p * cols : (p + 1) * cols]
            cycle = jnp.where(row_irrep == irrep_ref[pl.ds(block, 1), :], value, 0.0)
            update = cycle / (row_energy + energy_ref[pl.ds(block, 1), :])
            out_ref[:, pl.ds(pl.multiple_of(block * cols, cols), cols)] = update.astype(out_ref.dtype)

    def group_blocks(group):
        return [lax.rem(me_y + d, ny) for d in ring_order(ny)[group * ny // 2 : (group + 1) * ny // 2]]

    mask_amplitudes()

    spread = jnp.where(iota((occ_count, cols), 0) % occ_pair == iota((occ_count, cols), 1) // slab_second, 1.0, 0.0)
    own_row = iota((ny, occ_count), 1) // occ_pair == iota((ny, occ_count), 0)
    col_occ = jnp.dot(jnp.where(own_row, occ_row, 0.0), spread, preferred_element_type=jnp.float32)
    col_irrep = jnp.bitwise_xor(col_occ.astype(jnp.int32), b_irrep)
    hot = jnp.concatenate([jnp.where(col_irrep == g, 1.0, 0.0) for g in range(IRREPS)], axis=0)
    counted = jnp.dot(hot, before, preferred_element_type=jnp.float32)
    slot = jnp.zeros((ny, cols), jnp.float32)
    for g in range(IRREPS):
        slot = jnp.where(col_irrep == g, counted[g * ny : (g + 1) * ny], slot)
    most_ref[0, 0] = jnp.max(slot)
    copy_most = pltpu.make_async_copy(most_ref, most_hbm, in_sem.at[len(copies_in)])
    copy_most.start()
    irrep_ref[...] = col_irrep
    slot_ref[...] = slot.astype(jnp.int32)

    seat = iota((width, cols), 0)
    for group in range(2):
        for p, block in enumerate(group_blocks(group)):
            placing = jnp.where(slot_ref[pl.ds(block, 1), :] + p * slots == seat, 1.0, 0.0)
            place_ref[group, :, p * cols : (p + 1) * cols] = placing.astype(jnp.bfloat16)
    for copy in copies_in[7:]:
        copy.wait()
    b_energy = jnp.zeros((1, cols), jnp.float32)
    for b in range(slab_second):
        b_energy = jnp.where(b_at == b, virt_en_s[0, slab_s[0, 1] + b], b_energy)
    energy_ref[...] = jnp.dot(
        jnp.where(own_row, occ_en_v[...], 0.0), spread, precision=HIGHEST, preferred_element_type=jnp.float32
    ) - b_energy
    row_first = me_c * mine
    row_occ = me_y * occ_pair + row_first // slab_first
    row_virt = row_first % slab_first
    row_at = iota((mine, cols), 0)
    row_irrep = jnp.zeros((mine, cols), jnp.int32)
    row_energy = jnp.zeros((mine, cols), jnp.float32)
    for i in range(mine):
        a = slab_s[0, 0] + row_virt + i
        row_irrep = jnp.where(row_at == i, jnp.bitwise_xor(occ_s[0, row_occ], virt_s[0, a]), row_irrep)
        row_energy = jnp.where(row_at == i, occ_en_s[0, row_occ] - virt_en_s[0, a], row_energy)

    relayed(0)
    relay(1)
    arrived(2, (0,))
    send_y(2, 4, 0)
    send_y(2, 3, 0)
    arrived(2, (1,))
    send_y(2, 3, 1)
    arrived(1)
    relayed(1)
    if last > 1:
        relay(2)
    x_first = multiply(0)
    arrived(3)
    arrived(4, (0,))
    x_second = multiply(1)
    if last > 1:
        relayed(2)
    z_first = send_z(0, x_first)
    z_second = send_z(1, x_second)
    finish(0, z_first)
    copy_most.wait()
    for copy in y_copies + x_first + x_second + z_first + z_second:
        copy.wait_send()
    finish(1, z_second)


def contract(amplitudes, integrals, *small, slots, collective_id=0):
    ny = lax.axis_size("pair")
    nx = NX
    nz = lax.axis_size("contr") // (nx * CORES)
    rows, depth = amplitudes.shape
    cols = integrals.shape[1]
    mine = rows // (nx * nz * CORES)
    width = ny // 2 * slots
    vmem = pl.BlockSpec(memory_space=pltpu.VMEM)
    hbm = pl.BlockSpec(memory_space=pltpu.HBM)
    f32 = jnp.float32
    bf16 = jnp.bfloat16
    dma = pltpu.SemaphoreType.DMA
    return pl.pallas_call(
        functools.partial(kernel, ny, nx, nz, slots),
        out_shape=(
            jax.ShapeDtypeStruct((mine, cols * ny), bf16),
            jax.ShapeDtypeStruct((1, 1), f32),
            *(jax.ShapeDtypeStruct(array.shape, array.dtype) for array in small),
        ),
        in_specs=[hbm] * 7,
        out_specs=(vmem, hbm) + (vmem,) * 5,
        scratch_shapes=[
            pltpu.SMEM((1, 1), f32),
            pltpu.VMEM((rows, depth), bf16),
            pltpu.VMEM((depth, cols), bf16),
            *(pltpu.SMEM(array.shape, array.dtype) for array in small),
            pltpu.VMEM((ny, 2, slots, depth // 2), bf16),
            pltpu.VMEM((2, nx, width // 128, rows // nx, 128), f32),
            pltpu.VMEM((2, nx * CORES, mine * nz, width), f32),
            pltpu.VMEM((2, nx * CORES - 1, mine * nz, width), f32),
            pltpu.VMEM((2, nz, mine, width), f32),
            pltpu.VMEM((2, nz - 1, mine, width), f32),
            pltpu.VMEM((ny, cols), jnp.int32),
            pltpu.VMEM((ny, cols), jnp.int32),
            pltpu.VMEM((ny, cols), f32),
            pltpu.VMEM((2, width, ny // 2 * cols), bf16),
            dma((13,)),
            dma((2 * ny,)),
            dma((2 * ny,)),
            dma((2, nx * CORES - 1)),
            dma((2, nx * CORES - 1)),
            dma((2, nz - 1)),
            dma((2, nz - 1)),
            pltpu.SemaphoreType.REGULAR((3,)),
        ],
        compiler_params=pltpu.CompilerParams(
            collective_id=collective_id, has_side_effects=True, vmem_limit_bytes=60 * 1024 * 1024
        ),
        cost_estimate=pl.CostEstimate(
            flops=2 * rows * depth * width * 2, bytes_accessed=2 * depth * (rows + cols), transcendentals=0
        ),
    )(amplitudes, integrals, *small)


def body(amplitudes, integrals, *small):
    small = [array[None, :] for array in small]
    update, most, *small = contract(amplitudes, integrals, *small, slots=SLOTS, collective_id=0)
    return lax.cond(
        most[0, 0] > SLOTS - 1,
        lambda: contract(amplitudes, integrals, *small, slots=integrals.shape[1], collective_id=1)[0],
        lambda: update,
    )


def solution(mesh):
    in_specs = (P("pair", "contr"), P("contr", "pair"), P(), P(), P(), P(), P())
    out_specs = P(("pair", "contr"), None)
    return jax.shard_map(body, mesh=mesh, in_specs=in_specs, out_specs=out_specs, check_vma=False)
```

```python
import functools

import jax
import jax.numpy as jnp
from jax import lax
from jax.experimental import pallas as pl
from jax.experimental.pallas import tpu as pltpu
from jax.sharding import PartitionSpec as P

IRREPS = 8
NX = 4
CORES = 2
SLOTS = 32
HIGHEST = lax.Precision.HIGHEST
MESH = pl.DeviceIdType.MESH
NT = (((1,), (1,)), ((), ()))


def iota(shape, axis):
    return lax.broadcasted_iota(jnp.int32, shape, axis)


def ring_order(ny):
    order = [0]
    for step in range(1, ny // 2):
        order += [step, ny - step]
    return order + [ny // 2]


def kernel(
    ny, nx, nz, slots, a_hbm, w_hbm, occ_hbm, virt_hbm, occ_en_hbm, virt_en_hbm, slab_hbm,
    out_ref, most_hbm, occ_v, virt_v, occ_en_v, virt_en_v, slab_v,
    most_ref, a_ref, w_ref, occ_s, virt_s, occ_en_s, virt_en_s, slab_s,
    gath, part, xc_out, xc_in, z_out, z_in, irrep_ref, slot_ref, energy_ref, place_ref,
    in_sem, y_send, y_recv, xc_send, xc_recv, z_send, z_recv, known_sem,
):
    me_y = lax.axis_index("pair")
    me_c = lax.axis_index("contr")
    core = me_c % CORES
    me_z = (me_c // CORES) % nz
    me_x = me_c // (CORES * nz)
    rows, depth = a_ref.shape
    cols = w_ref.shape[1]
    half = depth // 2
    occ_count = occ_v.shape[1]
    virt_count = virt_v.shape[1]
    occ_pair = occ_count // ny
    slab_first = rows // occ_pair
    slab_second = cols // occ_pair
    mine = rows // (nx * nz * CORES)
    position = {d: p for p, d in enumerate(ring_order(ny))}
    width = ny // 2 * slots
    rows_x = rows // nx

    def at(x, z, k):
        return (x * nz + z) * CORES + k

    other = at(me_x, me_z, 1 - core)

    def x_peer(step):
        return at(lax.rem(me_x + step, nx), me_z, core)

    def z_peer(step):
        return at(me_x, lax.rem(me_z + step, nz), core)

    def near(count, *steps):
        return sorted({step % count for most in steps for step in (most, -most)} - {0}, key=lambda step: -min(step, count - step))

    barrier = pltpu.get_barrier_semaphore()
    greeted = [(lax.rem(me_y + step, ny), me_c) for step in near(ny, 1, 2)]
    greeted += [(me_y, other)]
    greeted += [(me_y, x_peer(step)) for step in near(nx, 1)]
    greeted += [(me_y, z_peer(step)) for step in near(nz, 1)]

    copies_in = [
        pltpu.make_async_copy(src, dst, in_sem.at[i])
        for i, (src, dst) in enumerate(
            [
                (occ_hbm, occ_v),
                (virt_hbm, virt_v),
                (slab_hbm, slab_s),
                (virt_hbm, virt_s),
                (occ_hbm, occ_s),
                (w_hbm, w_ref),
                (a_hbm, a_ref),
                (occ_en_hbm, occ_en_s),
                (virt_en_hbm, virt_en_s),
                (occ_en_hbm, occ_en_v),
                (virt_en_hbm, virt_en_v),
                (slab_hbm, slab_v),
            ]
        )
    ]
    for copy in copies_in:
        copy.start()
    copy_a = copies_in[6]

    for device in greeted:
        pl.semaphore_signal(barrier, inc=1, device_id=device, device_id_type=MESH)

    relays = [[x_peer(step) for step in near(nx, 1)], [other]]
    reach, level = 1, 0
    while 2 * reach <= nz // 2:
        relays += [[]] * (level == len(relays))
        relays[level] = relays[level] + [z_peer(step) for step in near(nz, reach)]
        reach, level = 2 * reach, level + 1
    last = len(relays) - 1

    def relay(level):
        for peer in relays[level]:
            pl.semaphore_signal(known_sem.at[level], inc=1, device_id=(me_y, peer), device_id_type=MESH)

    def relayed(level):
        pl.semaphore_wait(known_sem.at[level], len(relays[level]))

    own_spread = jnp.where(
        iota((occ_count, cols), 0) == me_y * occ_pair + iota((occ_count, cols), 1) // slab_second, 1.0, 0.0
    )
    before = jnp.where(iota((cols, cols), 0) < iota((cols, cols), 1), 1.0, 0.0)
    b_at = iota((1, cols), 1) % slab_second
    for copy in copies_in[:6]:
        copy.wait()
    b_irrep = jnp.zeros((1, cols), jnp.int32)
    for b in range(slab_second):
        b_irrep = jnp.where(b_at == b, virt_s[0, slab_s[0, 1] + b], b_irrep)
    occ_row = occ_v[...].astype(jnp.float32)
    own_occ = jnp.dot(occ_row, own_spread, preferred_element_type=jnp.float32)
    own_irrep = jnp.bitwise_xor(own_occ.astype(jnp.int32), b_irrep)
    own_hot = jnp.where(own_irrep == iota((IRREPS, cols), 0), 1.0, 0.0)
    own_counted = jnp.dot(own_hot, before, preferred_element_type=jnp.float32)
    own_slot = jnp.sum(own_hot * own_counted, axis=0, keepdims=True).astype(jnp.int32)
    local_occ = depth // virt_count
    kc_irrep = jnp.concatenate(
        [jnp.bitwise_xor(virt_v[...], occ_s[0, me_c * local_occ + k]) for k in range(local_occ)], axis=1
    )
    key = own_irrep * slots + own_slot
    pick = jnp.where(iota((IRREPS * slots, cols), 0) == key, 1.0, 0.0).astype(jnp.bfloat16)
    picked = lax.dot_general(pick, w_ref[...], NT, preferred_element_type=jnp.float32)
    kept = picked[:slots]
    for g in range(1, IRREPS):
        kept = jnp.where(kc_irrep == g, picked[g * slots : (g + 1) * slots], kept)
    kept = kept.astype(jnp.bfloat16)
    for h in range(2):
        gath[position[0], h] = kept[:, h * half : (h + 1) * half]

    pl.semaphore_wait(barrier, len(greeted))

    def y_copy(src, dst, h, step):
        return pltpu.make_async_remote_copy(
            src_ref=gath.at[position[src], h],
            dst_ref=gath.at[position[dst], h],
            send_sem=y_send.at[2 * dst + h],
            recv_sem=y_recv.at[2 * dst + h],
            device_id=(lax.rem(me_y + step % ny, ny), me_c),
            device_id_type=MESH,
        )

    y_copies = []

    def send_y(src, dst, turn):
        for sign in (1, -1):
            h = turn if sign == 1 else 1 - turn
            y_copies.append(y_copy(sign * src % ny, sign * dst % ny, h, sign * (src - dst)))
            y_copies[-1].start()

    def arrived(dst, turns=(0, 1)):
        for turn in turns:
            for sign in (1, -1):
                h = turn if sign == 1 else 1 - turn
                y_copy(sign * dst % ny, sign * dst % ny, h, 1).wait_recv()

    def whole_copy(sign):
        return pltpu.make_async_remote_copy(
            src_ref=gath.at[position[0]],
            dst_ref=gath.at[position[sign % ny]],
            send_sem=y_send.at[2 * (sign % ny)],
            recv_sem=y_recv.at[2 * (sign % ny)],
            device_id=(lax.rem(me_y - sign % ny + ny, ny), me_c),
            device_id_type=MESH,
        )

    send_y(0, 2, 0)
    send_y(0, 2, 1)
    whole_copies = [whole_copy(sign) for sign in (1, -1)]
    for copy in whole_copies:
        copy.start()
    y_copies += whole_copies
    relay(0)

    def mask_amplitudes():
        a_at = iota((slab_first, 128), 0)
        a_irrep = jnp.zeros((slab_first, 128), jnp.int32)
        for a in range(slab_first):
            a_irrep = jnp.where(a_at == a, virt_s[0, slab_s[0, 0] + a], a_irrep)
        copy_a.wait()

        def mask(i, carry):
            at_rows = pl.ds(pl.multiple_of(i * slab_first, slab_first), slab_first)
            row_irrep = jnp.bitwise_xor(a_irrep, occ_s[0, me_y * occ_pair + i])
            row_irrep = jnp.concatenate([row_irrep] * (depth // 128), axis=1)
            block = a_ref[at_rows, :].astype(jnp.float32)
            a_ref[at_rows, :] = jnp.where(row_irrep == kc_irrep, block, 0.0).astype(jnp.bfloat16)
            return carry

        lax.fori_loop(0, occ_pair, mask, 0)

    def far_first(count):
        return sorted(range(count), key=lambda step: -min(step, count - step))

    def multiply(group):
        first = group * ny // 2
        blocks = [gath[first : first + ny // 2, h].reshape(width, half) for h in range(2)]
        copies = []
        for p in far_first(nx):
            x = lax.rem(me_x + p, nx)
            at_rows = pl.ds(pl.multiple_of(x * rows_x, rows_x), rows_x)
            total = sum(
                lax.dot_general(
                    a_ref[at_rows, h * half : (h + 1) * half], blocks[h], NT, preferred_element_type=jnp.float32
                )
                for h in range(2)
            )
            for t in range(width // 128):
                part[group, p, t] = total[:, t * 128 : (t + 1) * 128]
            for k in range(CORES):
                for i in range(mine):
                    xc_out[group, p * CORES + k, i * nz : (i + 1) * nz] = strided(group, p, i, k)
            for q in range(CORES):
                if p or q:
                    k = lax.rem(core + q, CORES)
                    copies.append(
                        pltpu.make_async_remote_copy(
                            src_ref=xc_out.at[group, p * CORES + k],
                            dst_ref=xc_in.at[group, p * CORES + q - 1],
                            send_sem=xc_send.at[group, p * CORES + q - 1],
                            recv_sem=xc_recv.at[group, p * CORES + q - 1],
                            device_id=(me_y, at(x, me_z, k)),
                            device_id_type=MESH,
                        )
                    )
                    copies[-1].start()
        return copies

    def strided(group, p, i, k):
        at_rows = pl.ds(k * mine + i, nz, stride=CORES * mine)
        return jnp.concatenate([part[group, p, t, at_rows, :] for t in range(width // 128)], axis=1)

    def z_copy(group, step):
        return pltpu.make_async_remote_copy(
            src_ref=z_out.at[group, lax.rem(me_z + step, nz)],
            dst_ref=z_in.at[group, step - 1],
            send_sem=z_send.at[group, step - 1],
            recv_sem=z_recv.at[group, step - 1],
            device_id=(me_y, z_peer(step)),
            device_id_type=MESH,
        )

    def send_z(group, copies):
        total = xc_out[group, core]
        for copy in copies:
            copy.wait_recv()
        for step in range(nx * CORES - 1):
            total = total + xc_in[group, step].astype(jnp.float32)
        for i in range(mine):
            z_out[group, :, i, :] = total[i * nz : (i + 1) * nz]

        copies = [z_copy(group, step) for step in sorted(range(1, nz), key=lambda step: -min(step, nz - step))]
        for copy in copies:
            copy.start()
        return copies

    def finish(group, copies):
        for copy in copies:
            copy.wait_recv()
        total = z_out[group, me_z]
        for step in range(nz - 1):
            total = total + z_in[group, step]
        high = total.astype(jnp.bfloat16)
        rest = total - high.astype(jnp.float32)
        middle = rest.astype(jnp.bfloat16)
        low = (rest - middle.astype(jnp.float32)).astype(jnp.bfloat16)
        terms = jnp.concatenate([term.astype(jnp.float32) for term in (low, middle, high)], axis=0).astype(jnp.bfloat16)
        placed = jnp.dot(terms, place_ref[group], preferred_element_type=jnp.float32)
        placed = placed[:mine] + placed[mine : 2 * mine] + placed[2 * mine :]
        blocks = group_blocks(group)
        for p, block in enumerate(blocks):
            value = placed[:, p * cols : (p + 1) * cols]
            cycle = jnp.where(row_irrep == irrep_ref[pl.ds(block, 1), :], value, 0.0)
            update = cycle / (row_energy + energy_ref[pl.ds(block, 1), :])
            out_ref[:, pl.ds(pl.multiple_of(block * cols, cols), cols)] = update.astype(out_ref.dtype)

    def group_blocks(group):
        return [lax.rem(me_y + d, ny) for d in ring_order(ny)[group * ny // 2 : (group + 1) * ny // 2]]

    mask_amplitudes()

    relayed(0)
    relay(1)
    arrived(2, (0,))
    send_y(2, 4, 0)
    send_y(2, 3, 0)
    arrived(2, (1,))
    send_y(2, 3, 1)
    for copy in whole_copies:
        copy.wait_recv()
    relayed(1)
    if last > 1:
        relay(2)
    x_first = multiply(0)

    spread = jnp.where(iota((occ_count, cols), 0) % occ_pair == iota((occ_count, cols), 1) // slab_second, 1.0, 0.0)
    own_row = iota((ny, occ_count), 1) // occ_pair == iota((ny, occ_count), 0)
    col_occ = jnp.dot(jnp.where(own_row, occ_row, 0.0), spread, preferred_element_type=jnp.float32)
    col_irrep = jnp.bitwise_xor(col_occ.astype(jnp.int32), b_irrep)
    hot = jnp.concatenate([jnp.where(col_irrep == g, 1.0, 0.0) for g in range(IRREPS)], axis=0)
    counted = jnp.dot(hot, before, preferred_element_type=jnp.float32)
    slot = jnp.zeros((ny, cols), jnp.float32)
    for g in range(IRREPS):
        slot = jnp.where(col_irrep == g, counted[g * ny : (g + 1) * ny], slot)
    most_ref[0, 0] = jnp.max(slot)
    copy_most = pltpu.make_async_copy(most_ref, most_hbm, in_sem.at[len(copies_in)])
    copy_most.start()
    irrep_ref[...] = col_irrep
    slot_ref[...] = slot.astype(jnp.int32)

    seat = iota((width, cols), 0)
    for group in range(2):
        for p, block in enumerate(group_blocks(group)):
            placing = jnp.where(slot_ref[pl.ds(block, 1), :] + p * slots == seat, 1.0, 0.0)
            place_ref[group, :, p * cols : (p + 1) * cols] = placing.astype(jnp.bfloat16)
    for copy in copies_in[7:]:
        copy.wait()
    b_energy = jnp.zeros((1, cols), jnp.float32)
    for b in range(slab_second):
        b_energy = jnp.where(b_at == b, virt_en_s[0, slab_s[0, 1] + b], b_energy)
    energy_ref[...] = jnp.dot(
        jnp.where(own_row, occ_en_v[...], 0.0), spread, precision=HIGHEST, preferred_element_type=jnp.float32
    ) - b_energy
    row_first = me_c * mine
    row_occ = me_y * occ_pair + row_first // slab_first
    row_virt = row_first % slab_first
    row_at = iota((mine, cols), 0)
    row_irrep = jnp.zeros((mine, cols), jnp.int32)
    row_energy = jnp.zeros((mine, cols), jnp.float32)
    for i in range(mine):
        a = slab_s[0, 0] + row_virt + i
        row_irrep = jnp.where(row_at == i, jnp.bitwise_xor(occ_s[0, row_occ], virt_s[0, a]), row_irrep)
        row_energy = jnp.where(row_at == i, occ_en_s[0, row_occ] - virt_en_s[0, a], row_energy)

    arrived(3)
    arrived(4, (0,))
    x_second = multiply(1)
    if last > 1:
        relayed(2)
    z_first = send_z(0, x_first)
    z_second = send_z(1, x_second)
    finish(0, z_first)
    copy_most.wait()
    for copy in y_copies + x_first + x_second + z_first + z_second:
        copy.wait_send()
    finish(1, z_second)


def contract(amplitudes, integrals, *small, slots, collective_id=0):
    ny = lax.axis_size("pair")
    nx = NX
    nz = lax.axis_size("contr") // (nx * CORES)
    rows, depth = amplitudes.shape
    cols = integrals.shape[1]
    mine = rows // (nx * nz * CORES)
    width = ny // 2 * slots
    vmem = pl.BlockSpec(memory_space=pltpu.VMEM)
    hbm = pl.BlockSpec(memory_space=pltpu.HBM)
    f32 = jnp.float32
    bf16 = jnp.bfloat16
    dma = pltpu.SemaphoreType.DMA
    return pl.pallas_call(
        functools.partial(kernel, ny, nx, nz, slots),
        out_shape=(
            jax.ShapeDtypeStruct((mine, cols * ny), bf16),
            jax.ShapeDtypeStruct((1, 1), f32),
            *(jax.ShapeDtypeStruct(array.shape, array.dtype) for array in small),
        ),
        in_specs=[hbm] * 7,
        out_specs=(vmem, hbm) + (vmem,) * 5,
        scratch_shapes=[
            pltpu.SMEM((1, 1), f32),
            pltpu.VMEM((rows, depth), bf16),
            pltpu.VMEM((depth, cols), bf16),
            *(pltpu.SMEM(array.shape, array.dtype) for array in small),
            pltpu.VMEM((ny, 2, slots, depth // 2), bf16),
            pltpu.VMEM((2, nx, width // 128, rows // nx, 128), f32),
            pltpu.VMEM((2, nx * CORES, mine * nz, width), f32),
            pltpu.VMEM((2, nx * CORES - 1, mine * nz, width), f32),
            pltpu.VMEM((2, nz, mine, width), f32),
            pltpu.VMEM((2, nz - 1, mine, width), f32),
            pltpu.VMEM((ny, cols), jnp.int32),
            pltpu.VMEM((ny, cols), jnp.int32),
            pltpu.VMEM((ny, cols), f32),
            pltpu.VMEM((2, width, ny // 2 * cols), bf16),
            dma((13,)),
            dma((2 * ny,)),
            dma((2 * ny,)),
            dma((2, nx * CORES - 1)),
            dma((2, nx * CORES - 1)),
            dma((2, nz - 1)),
            dma((2, nz - 1)),
            pltpu.SemaphoreType.REGULAR((3,)),
        ],
        compiler_params=pltpu.CompilerParams(
            collective_id=collective_id, has_side_effects=True, vmem_limit_bytes=60 * 1024 * 1024
        ),
        cost_estimate=pl.CostEstimate(
            flops=2 * rows * depth * width * 2, bytes_accessed=2 * depth * (rows + cols), transcendentals=0
        ),
    )(amplitudes, integrals, *small)


def body(amplitudes, integrals, *small):
    small = [array[None, :] for array in small]
    update, most, *small = contract(amplitudes, integrals, *small, slots=SLOTS, collective_id=0)
    return lax.cond(
        most[0, 0] > SLOTS - 1,
        lambda: contract(amplitudes, integrals, *small, slots=integrals.shape[1], collective_id=1)[0],
        lambda: update,
    )


def solution(mesh):
    in_specs = (P("pair", "contr"), P("contr", "pair"), P(), P(), P(), P(), P())
    out_specs = P(("pair", "contr"), None)
    return jax.shard_map(body, mesh=mesh, in_specs=in_specs, out_specs=out_specs, check_vma=False)
```

```python
import functools

import jax
import jax.numpy as jnp
from jax import lax
from jax.experimental import pallas as pl
from jax.experimental.pallas import tpu as pltpu
from jax.sharding import PartitionSpec as P

IRREPS = 8
NX = 4
CORES = 2
SLOTS = 32
HIGHEST = lax.Precision.HIGHEST
MESH = pl.DeviceIdType.MESH
NT = (((1,), (1,)), ((), ()))


def iota(shape, axis):
    return lax.broadcasted_iota(jnp.int32, shape, axis)


def ring_order(ny):
    order = [0]
    for step in range(1, ny // 2):
        order += [step, ny - step]
    return order + [ny // 2]


def kernel(
    ny, nx, nz, slots, a_hbm, w_hbm, occ_hbm, virt_hbm, occ_en_hbm, virt_en_hbm, slab_hbm,
    out_ref, most_hbm, occ_v, virt_v, occ_en_v, virt_en_v, slab_v,
    most_ref, a_ref, w_ref, occ_s, virt_s, occ_en_s, virt_en_s, slab_s,
    gath, part, xc_out, xc_in, z_out, z_in, irrep_ref, slot_ref, energy_ref, place_ref,
    in_sem, y_send, y_recv, xc_send, xc_recv, z_send, z_recv, known_sem,
):
    me_y = lax.axis_index("pair")
    me_c = lax.axis_index("contr")
    core = me_c % CORES
    me_z = (me_c // CORES) % nz
    me_x = me_c // (CORES * nz)
    rows, depth = a_ref.shape
    cols = w_ref.shape[1]
    half = depth // 2
    occ_count = occ_v.shape[1]
    virt_count = virt_v.shape[1]
    occ_pair = occ_count // ny
    slab_first = rows // occ_pair
    slab_second = cols // occ_pair
    mine = rows // (nx * nz * CORES)
    position = {d: p for p, d in enumerate(ring_order(ny))}
    width = ny // 2 * slots
    rows_x = rows // nx

    def at(x, z, k):
        return (x * nz + z) * CORES + k

    other = at(me_x, me_z, 1 - core)

    def x_peer(step):
        return at(lax.rem(me_x + step, nx), me_z, core)

    def z_peer(step):
        return at(me_x, lax.rem(me_z + step, nz), core)

    def near(count, *steps):
        return sorted({step % count for most in steps for step in (most, -most)} - {0}, key=lambda step: -min(step, count - step))

    barrier = pltpu.get_barrier_semaphore()
    greeted = [(lax.rem(me_y + step, ny), me_c) for step in near(ny, 1, 2)]
    greeted += [(me_y, other)]
    greeted += [(me_y, x_peer(step)) for step in near(nx, 1)]
    greeted += [(me_y, z_peer(step)) for step in near(nz, 1)]

    copies_in = [
        pltpu.make_async_copy(src, dst, in_sem.at[i])
        for i, (src, dst) in enumerate(
            [
                (occ_hbm, occ_v),
                (virt_hbm, virt_v),
                (slab_hbm, slab_s),
                (virt_hbm, virt_s),
                (occ_hbm, occ_s),
                (w_hbm, w_ref),
                (a_hbm, a_ref),
                (occ_en_hbm, occ_en_s),
                (virt_en_hbm, virt_en_s),
                (occ_en_hbm, occ_en_v),
                (virt_en_hbm, virt_en_v),
                (slab_hbm, slab_v),
            ]
        )
    ]
    for copy in copies_in:
        copy.start()
    copy_a = copies_in[6]

    for device in greeted:
        pl.semaphore_signal(barrier, inc=1, device_id=device, device_id_type=MESH)

    relays = [[x_peer(step) for step in near(nx, 1)], [other]]
    reach, level = 1, 0
    while 2 * reach <= nz // 2:
        relays += [[]] * (level == len(relays))
        relays[level] = relays[level] + [z_peer(step) for step in near(nz, reach)]
        reach, level = 2 * reach, level + 1
    last = len(relays) - 1

    def relay(level):
        for peer in relays[level]:
            pl.semaphore_signal(known_sem.at[level], inc=1, device_id=(me_y, peer), device_id_type=MESH)

    def relayed(level):
        pl.semaphore_wait(known_sem.at[level], len(relays[level]))

    own_spread = jnp.where(
        iota((occ_count, cols), 0) == me_y * occ_pair + iota((occ_count, cols), 1) // slab_second, 1.0, 0.0
    )
    before = jnp.where(iota((cols, cols), 0) < iota((cols, cols), 1), 1.0, 0.0)
    b_at = iota((1, cols), 1) % slab_second
    for copy in copies_in[:6]:
        copy.wait()
    b_irrep = jnp.zeros((1, cols), jnp.int32)
    for b in range(slab_second):
        b_irrep = jnp.where(b_at == b, virt_s[0, slab_s[0, 1] + b], b_irrep)
    occ_row = occ_v[...].astype(jnp.float32)
    own_occ = jnp.dot(occ_row, own_spread, preferred_element_type=jnp.float32)
    own_irrep = jnp.bitwise_xor(own_occ.astype(jnp.int32), b_irrep)
    own_hot = jnp.where(own_irrep == iota((IRREPS, cols), 0), 1.0, 0.0)
    own_counted = jnp.dot(own_hot, before, preferred_element_type=jnp.float32)
    own_slot = jnp.sum(own_hot * own_counted, axis=0, keepdims=True).astype(jnp.int32)
    local_occ = depth // virt_count
    kc_irrep = jnp.concatenate(
        [jnp.bitwise_xor(virt_v[...], occ_s[0, me_c * local_occ + k]) for k in range(local_occ)], axis=1
    )
    key = own_irrep * slots + own_slot
    pick = jnp.where(iota((IRREPS * slots, cols), 0) == key, 1.0, 0.0).astype(jnp.bfloat16)
    picked = lax.dot_general(pick, w_ref[...], NT, preferred_element_type=jnp.float32)
    kept = picked[:slots]
    for g in range(1, IRREPS):
        kept = jnp.where(kc_irrep == g, picked[g * slots : (g + 1) * slots], kept)
    kept = kept.astype(jnp.bfloat16)
    for h in range(2):
        gath[position[0], h] = kept[:, h * half : (h + 1) * half]

    pl.semaphore_wait(barrier, len(greeted))

    def y_copy(src, dst, h, step):
        return pltpu.make_async_remote_copy(
            src_ref=gath.at[position[src], h],
            dst_ref=gath.at[position[dst], h],
            send_sem=y_send.at[2 * dst + h],
            recv_sem=y_recv.at[2 * dst + h],
            device_id=(lax.rem(me_y + step % ny, ny), me_c),
            device_id_type=MESH,
        )

    y_copies = []

    def send_y(src, dst, turn):
        for sign in (1, -1):
            h = turn if sign == 1 else 1 - turn
            y_copies.append(y_copy(sign * src % ny, sign * dst % ny, h, sign * (src - dst)))
            y_copies[-1].start()

    def arrived(dst, turns=(0, 1)):
        for turn in turns:
            for sign in (1, -1):
                h = turn if sign == 1 else 1 - turn
                y_copy(sign * dst % ny, sign * dst % ny, h, 1).wait_recv()

    def whole_copy(sign):
        return pltpu.make_async_remote_copy(
            src_ref=gath.at[position[0]],
            dst_ref=gath.at[position[sign % ny]],
            send_sem=y_send.at[2 * (sign % ny)],
            recv_sem=y_recv.at[2 * (sign % ny)],
            device_id=(lax.rem(me_y - sign % ny + ny, ny), me_c),
            device_id_type=MESH,
        )

    send_y(0, 2, 0)
    send_y(0, 2, 1)
    whole_copies = [whole_copy(sign) for sign in (1, -1)]
    for copy in whole_copies:
        copy.start()
    y_copies += whole_copies
    relay(0)

    def mask_amplitudes():
        a_at = iota((slab_first, 128), 0)
        a_irrep = jnp.zeros((slab_first, 128), jnp.int32)
        for a in range(slab_first):
            a_irrep = jnp.where(a_at == a, virt_s[0, slab_s[0, 0] + a], a_irrep)
        copy_a.wait()

        def mask(i, carry):
            at_rows = pl.ds(pl.multiple_of(i * slab_first, slab_first), slab_first)
            row_irrep = jnp.bitwise_xor(a_irrep, occ_s[0, me_y * occ_pair + i])
            row_irrep = jnp.concatenate([row_irrep] * (depth // 128), axis=1)
            block = a_ref[at_rows, :].astype(jnp.float32)
            a_ref[at_rows, :] = jnp.where(row_irrep == kc_irrep, block, 0.0).astype(jnp.bfloat16)
            return carry

        lax.fori_loop(0, occ_pair, mask, 0)

    def far_first(count):
        return sorted(range(count), key=lambda step: -min(step, count - step))

    def multiply(group):
        first = group * ny // 2
        blocks = [gath[first : first + ny // 2, h].reshape(width, half) for h in range(2)]
        copies = []
        for p in far_first(nx):
            x = lax.rem(me_x + p, nx)
            at_rows = pl.ds(pl.multiple_of(x * rows_x, rows_x), rows_x)
            total = sum(
                lax.dot_general(
                    a_ref[at_rows, h * half : (h + 1) * half], blocks[h], NT, preferred_element_type=jnp.float32
                )
                for h in range(2)
            )
            for t in range(width // 128):
                part[group, p, t] = total[:, t * 128 : (t + 1) * 128]
            for k in range(CORES):
                for i in range(mine):
                    xc_out[group, p * CORES + k, i * nz : (i + 1) * nz] = strided(group, p, i, k)
            for q in range(CORES):
                if p or q:
                    k = lax.rem(core + q, CORES)
                    copies.append(
                        pltpu.make_async_remote_copy(
                            src_ref=xc_out.at[group, p * CORES + k],
                            dst_ref=xc_in.at[group, p * CORES + q - 1],
                            send_sem=xc_send.at[group, p * CORES + q - 1],
                            recv_sem=xc_recv.at[group, p * CORES + q - 1],
                            device_id=(me_y, at(x, me_z, k)),
                            device_id_type=MESH,
                        )
                    )
                    copies[-1].start()
        return copies

    def strided(group, p, i, k):
        at_rows = pl.ds(k * mine + i, nz, stride=CORES * mine)
        return jnp.concatenate([part[group, p, t, at_rows, :] for t in range(width // 128)], axis=1)

    def z_copy(group, step):
        return pltpu.make_async_remote_copy(
            src_ref=z_out.at[group, lax.rem(me_z + step, nz)],
            dst_ref=z_in.at[group, step - 1],
            send_sem=z_send.at[group, step - 1],
            recv_sem=z_recv.at[group, step - 1],
            device_id=(me_y, z_peer(step)),
            device_id_type=MESH,
        )

    def send_z(group, copies):
        total = xc_out[group, core]
        steps = [p * CORES + q - 1 for p in far_first(nx) for q in range(CORES) if p or q]
        for copy, step in reversed(list(zip(copies, steps))):
            copy.wait_recv()
            total = total + xc_in[group, step]
        for i in range(mine):
            z_out[group, :, i, :] = total[i * nz : (i + 1) * nz]

        copies = [z_copy(group, step) for step in sorted(range(1, nz), key=lambda step: -min(step, nz - step))]
        for copy in copies:
            copy.start()
        return copies

    def finish(group, copies):
        for copy in copies:
            copy.wait_recv()
        total = z_out[group, me_z]
        for step in range(nz - 1):
            total = total + z_in[group, step]
        high = total.astype(jnp.bfloat16)
        rest = total - high.astype(jnp.float32)
        middle = rest.astype(jnp.bfloat16)
        low = (rest - middle.astype(jnp.float32)).astype(jnp.bfloat16)
        terms = jnp.concatenate([term.astype(jnp.float32) for term in (low, middle, high)], axis=0).astype(jnp.bfloat16)
        placed = jnp.dot(terms, place_ref[group], preferred_element_type=jnp.float32)
        placed = placed[:mine] + placed[mine : 2 * mine] + placed[2 * mine :]
        blocks = group_blocks(group)
        for p, block in enumerate(blocks):
            value = placed[:, p * cols : (p + 1) * cols]
            cycle = jnp.where(row_irrep == irrep_ref[pl.ds(block, 1), :], value, 0.0)
            update = cycle / (row_energy + energy_ref[pl.ds(block, 1), :])
            out_ref[:, pl.ds(pl.multiple_of(block * cols, cols), cols)] = update.astype(out_ref.dtype)

    def group_blocks(group):
        return [lax.rem(me_y + d, ny) for d in ring_order(ny)[group * ny // 2 : (group + 1) * ny // 2]]

    mask_amplitudes()

    relayed(0)
    relay(1)
    arrived(2, (0,))
    send_y(2, 4, 0)
    send_y(2, 3, 0)
    arrived(2, (1,))
    send_y(2, 3, 1)
    for copy in whole_copies:
        copy.wait_recv()
    relayed(1)
    if last > 1:
        relay(2)
    x_first = multiply(0)

    spread = jnp.where(iota((occ_count, cols), 0) % occ_pair == iota((occ_count, cols), 1) // slab_second, 1.0, 0.0)
    own_row = iota((ny, occ_count), 1) // occ_pair == iota((ny, occ_count), 0)
    col_occ = jnp.dot(jnp.where(own_row, occ_row, 0.0), spread, preferred_element_type=jnp.float32)
    col_irrep = jnp.bitwise_xor(col_occ.astype(jnp.int32), b_irrep)
    hot = jnp.concatenate([jnp.where(col_irrep == g, 1.0, 0.0) for g in range(IRREPS)], axis=0)
    counted = jnp.dot(hot, before, preferred_element_type=jnp.float32)
    slot = jnp.zeros((ny, cols), jnp.float32)
    for g in range(IRREPS):
        slot = jnp.where(col_irrep == g, counted[g * ny : (g + 1) * ny], slot)
    most_ref[0, 0] = jnp.max(slot)
    copy_most = pltpu.make_async_copy(most_ref, most_hbm, in_sem.at[len(copies_in)])
    copy_most.start()
    irrep_ref[...] = col_irrep
    slot_ref[...] = slot.astype(jnp.int32)

    seat = iota((width, cols), 0)
    for group in range(2):
        for p, block in enumerate(group_blocks(group)):
            placing = jnp.where(slot_ref[pl.ds(block, 1), :] + p * slots == seat, 1.0, 0.0)
            place_ref[group, :, p * cols : (p + 1) * cols] = placing.astype(jnp.bfloat16)
    for copy in copies_in[7:]:
        copy.wait()
    b_energy = jnp.zeros((1, cols), jnp.float32)
    for b in range(slab_second):
        b_energy = jnp.where(b_at == b, virt_en_s[0, slab_s[0, 1] + b], b_energy)
    energy_ref[...] = jnp.dot(
        jnp.where(own_row, occ_en_v[...], 0.0), spread, precision=HIGHEST, preferred_element_type=jnp.float32
    ) - b_energy
    row_first = me_c * mine
    row_occ = me_y * occ_pair + row_first // slab_first
    row_virt = row_first % slab_first
    row_at = iota((mine, cols), 0)
    row_irrep = jnp.zeros((mine, cols), jnp.int32)
    row_energy = jnp.zeros((mine, cols), jnp.float32)
    for i in range(mine):
        a = slab_s[0, 0] + row_virt + i
        row_irrep = jnp.where(row_at == i, jnp.bitwise_xor(occ_s[0, row_occ], virt_s[0, a]), row_irrep)
        row_energy = jnp.where(row_at == i, occ_en_s[0, row_occ] - virt_en_s[0, a], row_energy)

    arrived(3)
    arrived(4, (0,))
    x_second = multiply(1)
    if last > 1:
        relayed(2)
    z_first = send_z(0, x_first)
    z_second = send_z(1, x_second)
    finish(0, z_first)
    copy_most.wait()
    for copy in y_copies + x_first + x_second + z_first + z_second:
        copy.wait_send()
    finish(1, z_second)


def contract(amplitudes, integrals, *small, slots, collective_id=0):
    ny = lax.axis_size("pair")
    nx = NX
    nz = lax.axis_size("contr") // (nx * CORES)
    rows, depth = amplitudes.shape
    cols = integrals.shape[1]
    mine = rows // (nx * nz * CORES)
    width = ny // 2 * slots
    vmem = pl.BlockSpec(memory_space=pltpu.VMEM)
    hbm = pl.BlockSpec(memory_space=pltpu.HBM)
    f32 = jnp.float32
    bf16 = jnp.bfloat16
    dma = pltpu.SemaphoreType.DMA
    return pl.pallas_call(
        functools.partial(kernel, ny, nx, nz, slots),
        out_shape=(
            jax.ShapeDtypeStruct((mine, cols * ny), bf16),
            jax.ShapeDtypeStruct((1, 1), f32),
            *(jax.ShapeDtypeStruct(array.shape, array.dtype) for array in small),
        ),
        in_specs=[hbm] * 7,
        out_specs=(vmem, hbm) + (vmem,) * 5,
        scratch_shapes=[
            pltpu.SMEM((1, 1), f32),
            pltpu.VMEM((rows, depth), bf16),
            pltpu.VMEM((depth, cols), bf16),
            *(pltpu.SMEM(array.shape, array.dtype) for array in small),
            pltpu.VMEM((ny, 2, slots, depth // 2), bf16),
            pltpu.VMEM((2, nx, width // 128, rows // nx, 128), f32),
            pltpu.VMEM((2, nx * CORES, mine * nz, width), f32),
            pltpu.VMEM((2, nx * CORES - 1, mine * nz, width), f32),
            pltpu.VMEM((2, nz, mine, width), f32),
            pltpu.VMEM((2, nz - 1, mine, width), f32),
            pltpu.VMEM((ny, cols), jnp.int32),
            pltpu.VMEM((ny, cols), jnp.int32),
            pltpu.VMEM((ny, cols), f32),
            pltpu.VMEM((2, width, ny // 2 * cols), bf16),
            dma((13,)),
            dma((2 * ny,)),
            dma((2 * ny,)),
            dma((2, nx * CORES - 1)),
            dma((2, nx * CORES - 1)),
            dma((2, nz - 1)),
            dma((2, nz - 1)),
            pltpu.SemaphoreType.REGULAR((3,)),
        ],
        compiler_params=pltpu.CompilerParams(
            collective_id=collective_id, has_side_effects=True, vmem_limit_bytes=60 * 1024 * 1024
        ),
        cost_estimate=pl.CostEstimate(
            flops=2 * rows * depth * width * 2, bytes_accessed=2 * depth * (rows + cols), transcendentals=0
        ),
    )(amplitudes, integrals, *small)


def body(amplitudes, integrals, *small):
    small = [array[None, :] for array in small]
    update, most, *small = contract(amplitudes, integrals, *small, slots=SLOTS, collective_id=0)
    return lax.cond(
        most[0, 0] > SLOTS - 1,
        lambda: contract(amplitudes, integrals, *small, slots=integrals.shape[1], collective_id=1)[0],
        lambda: update,
    )


def solution(mesh):
    in_specs = (P("pair", "contr"), P("contr", "pair"), P(), P(), P(), P(), P())
    out_specs = P(("pair", "contr"), None)
    return jax.shard_map(body, mesh=mesh, in_specs=in_specs, out_specs=out_specs, check_vma=False)
```
